256 devices in a mesh: tensor: 8 (over z_hi, y), replica: 32 (over x, z_lo, core).
Axes of the slice: x: 4, y: 4, z: 8 (z_hi: 2, z_lo: 4; z = z_hi * 4 + z_lo), core: 2. Of those that a mesh axis runs over, the one named last changes fastest.
Arguments:
- tokens: bfloat16 [10240, 6144], P('replica', 'tensor'), may hold values from -6 to 6
- cotangent: bfloat16 [10240, 1024], P('replica', 'tensor'), may hold values from -6 to 6
- weights: bfloat16 [6144, 1024], P(None, 'tensor'), may hold values from -0.078125 to 0.078125
- momentum: float32 [32, 6144, 1024], P('replica', None, 'tensor'), may hold values from -6 to 6
Outputs:
- input_grad: bfloat16 [10240, 6144], P('replica', 'tensor')
- momentum_out: float32 [32, 6144, 1024], P('replica', None, 'tensor')
- update: float32 [6144, 1024], P(None, 'tensor')
The draws below stay inside these ranges and needn't reach their ends.
All inputs are finite; a program needn't handle non-finite values.
Results may differ from the reference program's by a relative error of at most 0.015.
Values may be sent and summed in bfloat16 or wider, within the bound.
A program may use at most 128 MiB of HBM per device.

```python
import math
import jax
import jax.numpy as jnp
from jax import lax

D = 6144
F = 1024
SPAN = 64
KEEP = 16
TOK_DEV = 320
REPLICAS = 32
TOKENS = 10240
N_TENSOR = 8
N_REPLICA = 32


def block_scale(own_key, dims, split, smallest, largest):
    factor_of = 1.0
    for dim, parts in split:
        heights = jax.random.uniform(jax.random.fold_in(jax.random.fold_in(own_key, 6), dim), (parts,), jnp.float32, smallest / len(split), largest / len(split))
        factor_of = factor_of * jnp.repeat(jnp.exp(heights), dims[dim] // parts).reshape((-1,) + (1,) * (len(dims) - 1 - dim))
    return factor_of


def gaussian(rng, dims, deviation, reach, shards=(), kind=jnp.bfloat16):
    array = deviation * jax.random.normal(rng, dims, jnp.float32)
    if shards:
        array = array * block_scale(rng, dims, shards, -0.22, 0.18)
    return jnp.clip(array, -reach, reach).astype(kind)


def setup_inputs(seed: int = 0) -> dict:
    splits = jax.random.split(jax.random.key(seed), 5)
    return {
        "tokens": gaussian(splits[0], (TOKENS, D), 1.0, 6.0, ((0, 32), (1, 8))),
        "cotangent": gaussian(splits[1], (TOKENS, F), 1.0, 6.0, ((0, 32), (1, 8))),
        "weights": gaussian(splits[2], (D, F), D ** -0.5, 0.078125, ((1, 8),)),
        "momentum": gaussian(splits[3], (REPLICAS, D, F), 1.0, 6.0, ((0, 32), (2, 8)), jnp.float32),
    }


decay_rate = 0.9

def cosine_table():
    order = jnp.arange(KEEP, dtype=jnp.float32)[:, None]
    place = jnp.arange(SPAN, dtype=jnp.float32)[None, :]
    table = jnp.cos(jnp.pi * (place + 0.5) * order / SPAN) * math.sqrt(2.0 / SPAN)
    return jnp.where(order == 0, table * math.sqrt(0.5), table)

def reference(tokens, cotangent, weights, momentum):
    table = cosine_table()
    width = weights.shape[1]
    group = width // N_TENSOR
    weight_groups = weights.astype(jnp.float32).reshape(D, N_TENSOR, group)

    def replica_step(items):
        rows, cotan, moment = items
        hidden = jnp.dot(rows, weights, preferred_element_type=jnp.float32)
        sig = jax.nn.sigmoid(hidden)
        grad_act = (cotan.astype(jnp.float32) * sig * (1.0 + hidden * (1.0 - sig))).astype(jnp.bfloat16)
        grad_w = lax.dot_general(rows, grad_act, (((0,), (0,)), ((), ())), preferred_element_type=jnp.float32) / math.sqrt(TOK_DEV)
        act_groups = grad_act.astype(jnp.float32).reshape(TOK_DEV, N_TENSOR, group)
        partial_terms = jnp.einsum('tgf,dgf->gtd', act_groups, weight_groups, precision=lax.Precision.HIGHEST)
        rounded = lax.optimization_barrier(partial_terms.astype(jnp.bfloat16))
        input_grad = lax.optimization_barrier(jnp.sum(rounded.astype(jnp.float32), axis=0)).astype(jnp.bfloat16)
        moment_new = decay_rate * moment + grad_w
        blocks = moment_new.reshape(D // SPAN, SPAN, width)
        coeffs = jnp.einsum('kj,cjf->ckf', table, blocks, precision=lax.Precision.HIGHEST)
        rest = blocks - jnp.einsum('kj,ckf->cjf', table, coeffs, precision=lax.Precision.HIGHEST)
        return (input_grad, rest.reshape(D, width), coeffs.astype(jnp.bfloat16))
    grads, moments, sent = lax.map(replica_step, (tokens.reshape(N_REPLICA, TOK_DEV, D), cotangent.reshape(N_REPLICA, TOK_DEV, width), momentum))
    total = lax.optimization_barrier(jnp.sum(sent.astype(jnp.float32), axis=0))
    update = jnp.einsum('kj,ckf->cjf', table, total, precision=lax.Precision.HIGHEST).reshape(D, width) / math.sqrt(N_REPLICA)
    return (grads.reshape(N_REPLICA * TOK_DEV, D), moments, update)
```

```python
import math

import jax
import jax.numpy as jnp
import numpy as np
from jax import lax
from jax.experimental import pallas as pl
from jax.experimental.pallas import tpu as pltpu
from jax.sharding import PartitionSpec as P

SPAN = 64
KEEP = 16
D = 6144
TOK = 320
COLS = 768
WIDTH = 128
CODED = 192
CHUNK = 256
DECAY = 0.9
MESH = pl.DeviceIdType.MESH
F32 = jnp.float32
BF16 = jnp.bfloat16


def cosine_table():
    order = np.arange(KEEP, dtype=np.float64)[:, None]
    place = np.arange(SPAN, dtype=np.float64)[None, :]
    table = np.cos(np.pi * (place + 0.5) * order / SPAN) * math.sqrt(2.0 / SPAN)
    return np.where(order == 0, table * math.sqrt(0.5), table)


def coder():
    table = cosine_table()
    four = np.eye(CHUNK // SPAN)
    rest = np.kron(four, np.eye(SPAN) - table.T @ table)
    return np.concatenate([rest, np.kron(four, table)], axis=0)


def decoder():
    return np.kron(np.eye(CHUNK // SPAN), cosine_table().T)


def position():
    t = lax.axis_index("tensor")
    r = lax.axis_index("replica")
    return r // 8, t % 4, t // 4, (r // 2) % 4, r % 2


def device(x, y, zh, zl, c):
    return (zh * 4 + y, (x * 4 + zl) * 2 + c)


def step_kernel(
    tok_h, cot_ref, w_h, mom_h, coder_ref,
    grad_out, mom_out, tot_out,
    gathered, w_v, mom_v, high_t, low_t, low_pre, hidden, act, w_rows,
    own, from_core, from_x, from_z, part_x, part_z, total,
    send, recv, local,
):
    x, y, zh, zl, c = position()
    yr, yl, yo = (y + 1) % 4, (y + 3) % 4, (y + 2) % 4
    zo = 1 - zh
    right, left, opp = device(x, yr, zh, zl, c), device(x, yl, zh, zl, c), device(x, yo, zh, zl, c)
    far = device(x, y, zo, zl, c)
    far_l, far_r, far_o = device(x, yl, zo, zl, c), device(x, yr, zo, zl, c), device(x, yo, zo, zl, c)
    sibling = device(x, y, zh, zl, 1 - c)
    xs = [(x + d) % 4 for d in (1, 2, 3)]
    zs = [(zl + d) % 4 for d in (1, 2, 3)]
    x_peers = [device(v, y, zh, zl, c) for v in xs]
    z_peers = [device(x, y, zh, v, c) for v in zs]
    shard = [zh * 4 + v for v in (y, yl, yr, yo)] + [zo * 4 + v for v in (y, yl, yr, yo)]
    tensor_peers = [None, left, right, opp, far, far_l, far_r, far_o]

    counter = iter(range(1000))

    def remote(src, dst, target):
        k = next(counter)
        return pltpu.make_async_remote_copy(
            src_ref=src, dst_ref=dst, send_sem=send.at[k], recv_sem=recv.at[k],
            device_id=target, device_id_type=MESH,
        )

    barrier = pltpu.get_barrier_semaphore()
    partners = tensor_peers[1:] + [sibling] + x_peers + z_peers
    for p in partners:
        pl.semaphore_signal(barrier, inc=1, device_id=p, device_id_type=MESH)

    tok_in = pltpu.make_async_copy(tok_h, gathered.at[0], local.at[0])
    tok_in.start()
    w_in = pltpu.make_async_copy(w_h, w_v, local.at[1])
    w_in.start()
    mom_in = pltpu.make_async_copy(mom_h, mom_v, local.at[2])
    mom_in.start()
    hidden[...] = jnp.zeros_like(hidden)

    pl.semaphore_wait(barrier, len(partners))

    outgoing = []

    def go(copy):
        copy.start()
        outgoing.append(copy)
        return copy

    half = TOK // 2
    piece = 64
    pieces = TOK // piece
    far_in = []
    first = pl.ds(0, half)
    second = pl.ds(half, half)
    far_in.append(go(remote(tok_h.at[pl.ds(0, piece)], gathered.at[4, pl.ds(0, piece)], far)))
    from_l1 = go(remote(tok_h.at[first], gathered.at[1, first], right))
    from_r2 = go(remote(tok_h.at[second], gathered.at[2, second], left))
    for i in range(1, pieces):
        rows = pl.ds(i * piece, piece)
        far_in.append(go(remote(tok_h.at[rows], gathered.at[4, rows], far)))
    from_l2 = go(remote(tok_h.at[second], gathered.at[1, second], right))
    from_r1 = go(remote(tok_h.at[first], gathered.at[2, first], left))

    w_in.wait()
    w_copies = []
    mirror = [0, 2, 1, 3, 4, 6, 5, 7]
    share = 2 * x + c
    for s in range(1, 8):
        rows = pl.ds(pl.multiple_of(shard[s] * COLS + share * 96, 32), 96)
        w_copies.append(
            go(remote(w_v.at[rows], w_rows.at[mirror[s], share], tensor_peers[s]))
        )

    def process(slot):
        rows = pl.ds(pl.multiple_of(shard[slot] * COLS, COLS), COLS)
        hidden[...] += jnp.dot(gathered[slot], w_v[rows, :], preferred_element_type=F32)
        for j in range(COLS // CHUNK):
            coded = lax.dot_general(
                coder_ref[...], gathered[slot, :, j * CHUNK:(j + 1) * CHUNK],
                (((1,), (1,)), ((), ())), preferred_element_type=F32,
            ).astype(BF16)
            high_t[pl.ds(slot * COLS + j * CHUNK, CHUNK), :] = coded[:CHUNK]
            low_t[pl.ds(slot * CODED + j * SPAN, SPAN), :] = coded[CHUNK:]

    def momentum_pre(slot):
        def chunk(j, carry):
            rows = pl.ds(pl.multiple_of(shard[slot] * COLS + j * CHUNK, CHUNK), CHUNK)
            coded = DECAY * jnp.dot(
                coder_ref[...], mom_v[rows, :].astype(BF16), preferred_element_type=F32
            )
            mom_v[rows, :] = coded[:CHUNK]
            low_pre[pl.ds(pl.multiple_of(slot * CODED + j * SPAN, SPAN), SPAN), :] = coded[CHUNK:]
            return carry
        lax.fori_loop(0, COLS // CHUNK, chunk, 0)

    tok_in.wait()
    process(0)
    mom_in.wait()
    for s in range(3):
        momentum_pre(s)

    far_fwd_r, far_fwd_l, far_opp = [], [], []

    def forward_far(i):
        rows = pl.ds(i * piece, piece)
        far_in[i].wait_recv()
        far_fwd_r.append(go(remote(gathered.at[4, rows], gathered.at[5, rows], right)))
        far_fwd_l.append(go(remote(gathered.at[4, rows], gathered.at[6, rows], left)))

    def forward_far_opp(i):
        lower = pl.ds(i * piece, piece // 2)
        upper = pl.ds(i * piece + piece // 2, piece // 2)
        far_fwd_r[i].wait_recv()
        far_opp.append(go(remote(gathered.at[5, lower], gathered.at[7, lower], right)))
        far_fwd_l[i].wait_recv()
        far_opp.append(go(remote(gathered.at[6, upper], gathered.at[7, upper], left)))

    from_l1.wait_recv()
    opp1 = go(remote(gathered.at[1, first], gathered.at[3, first], right))
    from_r2.wait_recv()
    opp2 = go(remote(gathered.at[2, second], gathered.at[3, second], left))
    forward_far(0)
    momentum_pre(3)
    momentum_pre(4)
    for w in w_copies:
        w.wait_recv()
    mine = w_rows.at[pl.ds(1, 7), share]
    w_x = [go(remote(mine, mine, p)) for p in x_peers]
    from_l2.wait_recv()
    process(1)
    from_r1.wait_recv()
    process(2)
    forward_far(1)
    momentum_pre(5)
    momentum_pre(6)
    forward_far(2)
    opp1.wait_recv()
    opp2.wait_recv()
    process(3)
    momentum_pre(7)
    forward_far_opp(0)
    forward_far(3)
    forward_far_opp(1)
    forward_far(4)
    process(4)
    for w in w_x:
        w.wait_recv()
    w_core = []
    for v in range(4):
        block = w_rows.at[pl.ds(1, 7), 2 * v + c]
        w_core.append(go(remote(block, block, sibling)))
    own_rows = pl.ds(pl.multiple_of(shard[0] * COLS, COLS), COLS)
    w_rows[0] = w_v[own_rows, :].reshape(8, 96, WIDTH)
    forward_far_opp(2)
    forward_far_opp(3)
    forward_far_opp(4)
    process(5)
    process(6)
    for copy in far_opp:
        copy.wait_recv()
    process(7)

    h = hidden[...]
    sig = jax.nn.sigmoid(h)
    act[0] = (cot_ref[...].astype(F32) * sig * (1.0 + h * (1.0 - sig))).astype(BF16)
    act_far = go(remote(act.at[0], act.at[4], far))

    inv = 1.0 / math.sqrt(TOK)
    lower_half = D // SPAN * KEEP // 2

    def code(base):
        def chunk(j, carry):
            rows = pl.ds(pl.multiple_of(base + j * CHUNK, CHUNK), CHUNK)
            grad = jnp.dot(low_t[rows, :], act[0], preferred_element_type=F32)
            own[rows, :] = (low_pre[rows, :] + grad * inv).astype(BF16)
            return carry
        lax.fori_loop(0, lower_half // CHUNK, chunk, 0)

    code((1 - c) * lower_half)
    theirs = pl.ds(pl.multiple_of((1 - c) * lower_half, lower_half), lower_half)
    mine_rows = pl.ds(pl.multiple_of(c * lower_half, lower_half), lower_half)
    red_core = go(remote(own.at[theirs], from_core, sibling))
    act_l = go(remote(act.at[0], act.at[1], right))
    act_r = go(remote(act.at[0], act.at[2], left))
    act_o = go(remote(act.at[0], act.at[3], opp))
    code(c * lower_half)

    mom_copies = []

    def momentum_post(slot):
        def chunk(j, carry):
            rows = pl.ds(pl.multiple_of(shard[slot] * COLS + j * CHUNK, CHUNK), CHUNK)
            t_rows = pl.ds(pl.multiple_of(slot * COLS + j * CHUNK, CHUNK), CHUNK)
            grad = jnp.dot(high_t[t_rows, :], act[0], preferred_element_type=F32)
            mom_v[rows, :] = mom_v[rows, :] + grad * inv
            return carry
        lax.fori_loop(0, COLS // CHUNK, chunk, 0)
        rows = pl.ds(pl.multiple_of(shard[slot] * COLS, COLS), COLS)
        copy = pltpu.make_async_copy(mom_v.at[rows], mom_out.at[rows], local.at[4 + slot])
        copy.start()
        mom_copies.append(copy)

    momentum_post(0)
    red_core.wait_recv()
    part_x[...] = (
        own[mine_rows, :].astype(F32) + from_core[...].astype(F32)
    ).astype(BF16).reshape(4, CODED, WIDTH)
    red_x = [
        go(remote(part_x.at[v], from_x.at[i], p)) for i, (v, p) in enumerate(zip(xs, x_peers))
    ]
    momentum_post(1)
    momentum_post(2)
    momentum_post(3)
    for copy in red_x:
        copy.wait_recv()
    summed = part_x[x].astype(F32)
    for i in range(3):
        summed = summed + from_x[i].astype(F32)
    part_z[...] = summed.astype(BF16).reshape(4, 48, WIDTH)
    red_z = [
        go(remote(part_z.at[v], from_z.at[i], p)) for i, (v, p) in enumerate(zip(zs, z_peers))
    ]
    act_far.wait_recv()
    act_fl = go(remote(act.at[4], act.at[5], right))
    act_fr = go(remote(act.at[4], act.at[6], left))
    act_fo = go(remote(act.at[4], act.at[7], opp))
    momentum_post(4)
    momentum_post(5)
    for copy in red_z:
        copy.wait_recv()
    summed = part_z[zl].astype(F32)
    for i in range(3):
        summed = summed + from_z[i].astype(F32)
    total[c, x, zl] = summed.astype(BF16)
    spread_z = [go(remote(total.at[c, x, zl], total.at[c, x, zl], p)) for p in z_peers]
    momentum_post(6)
    momentum_post(7)
    for copy in spread_z:
        copy.wait_recv()
    spread_x = [go(remote(total.at[c, x], total.at[c, x], p)) for p in x_peers]

    for copy in w_core + [act_l, act_r, act_o, act_fl, act_fr, act_fo]:
        copy.wait_recv()

    def input_grad(j, carry):
        rows = pl.ds(pl.multiple_of(j * 64, 64), 64)
        acc = jnp.zeros((64, COLS), F32)
        for s in range(8):
            acc = acc + lax.dot_general(
                act[s, rows, :], w_rows[s].reshape(COLS, WIDTH),
                (((1,), (1,)), ((), ())), preferred_element_type=F32,
            )
        grad_out[rows, :] = acc.astype(BF16)
        return carry

    lax.fori_loop(0, TOK // 64, input_grad, 0)

    for copy in spread_x:
        copy.wait_recv()
    spread_core = go(remote(total.at[c], total.at[c], sibling))
    spread_core.wait_recv()
    tot_copies = []
    for s in range(8):
        src = total.at[s // 4, s % 4]
        dst = tot_out.at[shard[s]]
        copy = pltpu.make_async_copy(src, dst, local.at[12 + s])
        copy.start()
        tot_copies.append(copy)
    for copy in mom_copies + tot_copies:
        copy.wait()
    for copy in outgoing:
        copy.wait_send()


def decode_kernel(scale, total_ref, decoder_ref, out_ref):
    for j in range(COLS // CHUNK):
        out_ref[pl.ds(j * CHUNK, CHUNK), :] = scale * jnp.dot(
            decoder_ref[...], total_ref[0, pl.ds(j * SPAN, SPAN), :],
            preferred_element_type=F32,
        )


def per_device(tokens, cotangent, weights, momentum):
    replicas = lax.axis_size("replica")
    coder_c = jnp.asarray(coder(), F32).astype(BF16)
    decoder_c = jnp.asarray(decoder(), F32).astype(BF16)
    vmem = pl.BlockSpec(memory_space=pltpu.VMEM)
    hbm = pl.BlockSpec(memory_space=pl.ANY)
    copies = 80
    input_grad, momentum_out, total = pl.pallas_call(
        step_kernel,
        out_shape=(
            jax.ShapeDtypeStruct((TOK, COLS), BF16),
            jax.ShapeDtypeStruct((D, WIDTH), F32),
            jax.ShapeDtypeStruct((8, 4, 48, WIDTH), BF16),
        ),
        in_specs=[hbm, vmem, hbm, hbm, vmem],
        out_specs=(vmem, hbm, hbm),
        scratch_shapes=[
            pltpu.VMEM((8, TOK, COLS), BF16),
            pltpu.VMEM((D, WIDTH), BF16),
            pltpu.VMEM((D, WIDTH), F32),
            pltpu.VMEM((D, TOK), BF16),
            pltpu.VMEM((8 * CODED, TOK), BF16),
            pltpu.VMEM((8 * CODED, WIDTH), F32),
            pltpu.VMEM((TOK, WIDTH), F32),
            pltpu.VMEM((8, TOK, WIDTH), BF16),
            pltpu.VMEM((8, 8, 96, WIDTH), BF16),
            pltpu.VMEM((8 * CODED, WIDTH), BF16),
            pltpu.VMEM((4 * CODED, WIDTH), BF16),
            pltpu.VMEM((3, CODED, WIDTH), BF16),
            pltpu.VMEM((3, 48, WIDTH), BF16),
            pltpu.VMEM((4, CODED, WIDTH), BF16),
            pltpu.VMEM((4, 48, WIDTH), BF16),
            pltpu.VMEM((2, 4, 4, 48, WIDTH), BF16),
            pltpu.SemaphoreType.DMA((copies,)),
            pltpu.SemaphoreType.DMA((copies,)),
            pltpu.SemaphoreType.DMA((20,)),
        ],
        compiler_params=pltpu.CompilerParams(
            collective_id=0, has_side_effects=True, vmem_limit_bytes=56 << 20
        ),
        name="step",
    )(tokens, cotangent, weights, momentum[0], coder_c)
    total = total.reshape(8, CODED, WIDTH)
    update = pl.pallas_call(
        lambda *refs: decode_kernel(1.0 / math.sqrt(replicas), *refs),
        grid=(8,),
        out_shape=jax.ShapeDtypeStruct((D, WIDTH), F32),
        in_specs=[
            pl.BlockSpec((1, CODED, WIDTH), lambda i: (i, 0, 0)),
            pl.BlockSpec((CHUNK, SPAN), lambda i: (0, 0)),
        ],
        out_specs=pl.BlockSpec((COLS, WIDTH), lambda i: (i, 0)),
        name="decode",
    )(total, decoder_c)
    return input_grad, momentum_out[None], update


def solution(mesh):
    in_specs = (
        P("replica", "tensor"),
        P("replica", "tensor"),
        P(None, "tensor"),
        P("replica", None, "tensor"),
    )
    out_specs = (P("replica", "tensor"), P("replica", None, "tensor"), P(None, "tensor"))
    return jax.shard_map(
        per_device, mesh=mesh, in_specs=in_specs, out_specs=out_specs, check_vma=False
    )
```

```python
import math

import jax
import jax.numpy as jnp
import numpy as np
from jax import lax
from jax.experimental import pallas as pl
from jax.experimental.pallas import tpu as pltpu
from jax.sharding import PartitionSpec as P

SPAN = 64
KEEP = 16
D = 6144
TOK = 320
COLS = 768
WIDTH = 128
CODED = 192
CHUNK = 256
DECAY = 0.9
MESH = pl.DeviceIdType.MESH
F32 = jnp.float32
BF16 = jnp.bfloat16


def cosine_table():
    order = np.arange(KEEP, dtype=np.float64)[:, None]
    place = np.arange(SPAN, dtype=np.float64)[None, :]
    table = np.cos(np.pi * (place + 0.5) * order / SPAN) * math.sqrt(2.0 / SPAN)
    return np.where(order == 0, table * math.sqrt(0.5), table)


def coder():
    table = cosine_table()
    four = np.eye(CHUNK // SPAN)
    rest = np.kron(four, np.eye(SPAN) - table.T @ table)
    return np.concatenate([rest, np.kron(four, table)], axis=0)


def decoder():
    return np.kron(np.eye(CHUNK // SPAN), cosine_table().T)


def position():
    t = lax.axis_index("tensor")
    r = lax.axis_index("replica")
    return r // 8, t % 4, t // 4, (r // 2) % 4, r % 2


def device(x, y, zh, zl, c):
    return (zh * 4 + y, (x * 4 + zl) * 2 + c)


def step_kernel(
    tok_h, cot_ref, w_h, mom_h, coder_ref,
    grad_out, mom_out, tot_out,
    gathered, w_v, mom_v, high_t, low_t, low_pre, hidden, act, w_rows,
    to_core, from_core, part_x, kept_x, from_x, part_z, to_z, from_z,
    send, recv, local,
):
    x, y, zh, zl, c = position()
    yr, yl, yo = (y + 1) % 4, (y + 3) % 4, (y + 2) % 4
    zo = 1 - zh
    right, left, opp = device(x, yr, zh, zl, c), device(x, yl, zh, zl, c), device(x, yo, zh, zl, c)
    far = device(x, y, zo, zl, c)
    far_l, far_r, far_o = device(x, yl, zo, zl, c), device(x, yr, zo, zl, c), device(x, yo, zo, zl, c)
    sibling = device(x, y, zh, zl, 1 - c)
    xs = [(x + d) % 4 for d in (1, 2, 3)]
    zs = [(zl + d) % 4 for d in (1, 2, 3)]
    x_peers = [device(v, y, zh, zl, c) for v in xs]
    z_peers = [device(x, y, zh, v, c) for v in zs]
    shard = [zh * 4 + v for v in (y, yl, yr, yo)] + [zo * 4 + v for v in (y, yl, yr, yo)]
    tensor_peers = [None, left, right, opp, far, far_l, far_r, far_o]

    counter = iter(range(1000))

    def remote(src, dst, target):
        k = next(counter)
        return pltpu.make_async_remote_copy(
            src_ref=src, dst_ref=dst, send_sem=send.at[k], recv_sem=recv.at[k],
            device_id=target, device_id_type=MESH,
        )

    barrier = pltpu.get_barrier_semaphore()
    partners = tensor_peers[1:] + [sibling] + x_peers + z_peers
    for p in partners:
        pl.semaphore_signal(barrier, inc=1, device_id=p, device_id_type=MESH)

    tok_in = pltpu.make_async_copy(tok_h, gathered.at[0], local.at[0])
    tok_in.start()
    w_in = pltpu.make_async_copy(w_h, w_v, local.at[1])
    w_in.start()
    mom_in = pltpu.make_async_copy(mom_h, mom_v, local.at[2])
    mom_in.start()
    hidden[...] = jnp.zeros_like(hidden)

    pl.semaphore_wait(barrier, len(partners))

    outgoing = []

    def go(copy):
        copy.start()
        outgoing.append(copy)
        return copy

    def process(slot):
        rows = pl.ds(pl.multiple_of(shard[slot] * COLS, COLS), COLS)
        hidden[...] += jnp.dot(gathered[slot], w_v[rows, :], preferred_element_type=F32)
        for j in range(COLS // CHUNK):
            coded = lax.dot_general(
                coder_ref[...], gathered[slot, :, j * CHUNK:(j + 1) * CHUNK],
                (((1,), (1,)), ((), ())), preferred_element_type=F32,
            ).astype(BF16)
            high_t[pl.ds(slot * COLS + j * CHUNK, CHUNK), :] = coded[:CHUNK]
            low_t[pl.ds(slot * CODED + j * SPAN, SPAN), :] = coded[CHUNK:]

    def momentum_pre(slot):
        def chunk(j, carry):
            rows = pl.ds(pl.multiple_of(shard[slot] * COLS + j * CHUNK, CHUNK), CHUNK)
            slot_rows = pl.ds(pl.multiple_of(slot * COLS + j * CHUNK, CHUNK), CHUNK)
            coded = DECAY * jnp.dot(
                coder_ref[...], mom_v[rows, :].astype(BF16), preferred_element_type=F32
            )
            mom_out[slot_rows, :] = coded[:CHUNK]
            low_pre[pl.ds(pl.multiple_of(slot * CODED + j * SPAN, SPAN), SPAN), :] = coded[CHUNK:]
            return carry
        lax.fori_loop(0, COLS // CHUNK, chunk, 0)
    half = TOK // 2
    piece = 64
    pieces = TOK // piece
    first = pl.ds(0, half)
    second = pl.ds(half, half)
    far_in, far_fwd_r, far_fwd_l, far_opp = [], [], [], []

    def send_far(i):
        rows = pl.ds(i * piece, piece)
        far_in.append(go(remote(tok_h.at[rows], gathered.at[4, rows], far)))

    def forward_far(i):
        rows = pl.ds(i * piece, piece)
        far_in[i].wait_recv()
        if i + 2 < pieces:
            send_far(i + 2)
        far_fwd_r.append(go(remote(gathered.at[4, rows], gathered.at[5, rows], right)))
        far_fwd_l.append(go(remote(gathered.at[4, rows], gathered.at[6, rows], left)))

    def forward_far_opp(i):
        lower = pl.ds(i * piece, piece // 2)
        upper = pl.ds(i * piece + piece // 2, piece // 2)
        far_fwd_r[i].wait_recv()
        far_opp.append(go(remote(gathered.at[5, lower], gathered.at[7, lower], right)))
        far_fwd_l[i].wait_recv()
        far_opp.append(go(remote(gathered.at[6, upper], gathered.at[7, upper], left)))

    send_far(0)
    from_l1 = go(remote(tok_h.at[first], gathered.at[1, first], right))
    from_r2 = go(remote(tok_h.at[second], gathered.at[2, second], left))
    send_far(1)
    from_l2 = go(remote(tok_h.at[second], gathered.at[1, second], right))
    from_r1 = go(remote(tok_h.at[first], gathered.at[2, first], left))

    w_in.wait()
    tok_in.wait()
    process(0)
    mom_in.wait()
    momentum_pre(0)
    momentum_pre(1)
    forward_far(0)
    momentum_pre(2)
    momentum_pre(3)
    forward_far(1)
    momentum_pre(4)
    from_l1.wait_recv()
    opp1 = go(remote(gathered.at[1, first], gathered.at[3, first], right))
    from_r2.wait_recv()
    opp2 = go(remote(gathered.at[2, second], gathered.at[3, second], left))
    momentum_pre(5)
    forward_far(2)
    from_l2.wait_recv()
    process(1)
    forward_far_opp(0)
    from_r1.wait_recv()
    process(2)
    forward_far(3)
    momentum_pre(6)
    forward_far_opp(1)
    momentum_pre(7)
    forward_far(4)
    w_copies = []
    mirror = [0, 2, 1, 3, 4, 6, 5, 7]
    share = 2 * x + c
    for s in range(1, 8):
        rows = pl.ds(pl.multiple_of(shard[s] * COLS + share * 96, 32), 96)
        w_copies.append(
            go(remote(w_v.at[rows], w_rows.at[mirror[s], share], tensor_peers[s]))
        )
    forward_far_opp(2)
    process(4)
    forward_far_opp(3)
    opp1.wait_recv()
    opp2.wait_recv()
    process(3)
    forward_far_opp(4)
    process(5)
    process(6)
    for w in w_copies:
        w.wait_recv()
    mine = w_rows.at[pl.ds(1, 7), share]
    w_x = [go(remote(mine, mine, p)) for p in x_peers]
    for copy in far_opp:
        copy.wait_recv()
    process(7)

    h = hidden[...]
    sig = jax.nn.sigmoid(h)
    act[0] = (cot_ref[...].astype(F32) * sig * (1.0 + h * (1.0 - sig))).astype(BF16)
    act_far = go(remote(act.at[0], act.at[4], far))

    inv = 1.0 / math.sqrt(TOK)

    def code(slot):
        rows = pl.ds(pl.multiple_of(slot * CODED, CODED), CODED)
        grad = jnp.dot(low_t[rows, :], act[0], preferred_element_type=F32)
        return low_pre[rows, :] + grad * inv

    def momentum_post(slot):
        def chunk(j, carry):
            rows = pl.ds(pl.multiple_of(slot * COLS + j * CHUNK, CHUNK), CHUNK)
            grad = jnp.dot(high_t[rows, :], act[0], preferred_element_type=F32)
            mom_out[rows, :] = mom_out[rows, :] + grad * inv
            return carry
        lax.fori_loop(0, COLS // CHUNK, chunk, 0)

    order = [xs[1], xs[0], xs[2], x]
    red_core = []
    for i, v in enumerate(order):
        to_core[i] = code((1 - c) * 4 + v).astype(BF16)
        red_core.append(go(remote(to_core.at[i], from_core.at[i], sibling)))
    red_x = []
    peers_of = [x_peers[1], x_peers[0], x_peers[2]]
    for i, v in enumerate(order):
        mine_q = code(c * 4 + v)
        red_core[i].wait_recv()
        both = mine_q + from_core[i].astype(F32)
        if i < 3:
            part_x[i] = both.astype(BF16)
            red_x.append(go(remote(part_x.at[i], from_x.at[i], peers_of[i])))
        else:
            kept_x[...] = both
    act_l = go(remote(act.at[0], act.at[1], right))
    act_r = go(remote(act.at[0], act.at[2], left))
    act_o = go(remote(act.at[0], act.at[3], opp))
    for w in w_x:
        w.wait_recv()
    w_core = []
    for v in range(4):
        block = w_rows.at[pl.ds(1, 7), 2 * v + c]
        w_core.append(go(remote(block, block, sibling)))
    momentum_post(0)
    momentum_post(1)
    momentum_post(2)
    for copy in red_x:
        copy.wait_recv()
    part_z[...] = (
        kept_x[...] + from_x[0].astype(F32) + from_x[1].astype(F32) + from_x[2].astype(F32)
    ).reshape(4, 48, WIDTH)
    to_z[...] = part_z[...].astype(BF16)
    red_z = [
        go(remote(to_z.at[v], from_z.at[i], p)) for i, (v, p) in enumerate(zip(zs, z_peers))
    ]
    act_far.wait_recv()
    act_fl = go(remote(act.at[4], act.at[5], right))
    act_fr = go(remote(act.at[4], act.at[6], left))
    act_fo = go(remote(act.at[4], act.at[7], opp))
    momentum_post(3)
    momentum_post(4)
    for copy in red_z:
        copy.wait_recv()
    tot_out[c, x, zl] = (
        part_z[zl] + from_z[0].astype(F32) + from_z[1].astype(F32) + from_z[2].astype(F32)
    ).astype(BF16)
    piece_ref = tot_out.at[c, x, zl]
    spread_z = [go(remote(piece_ref, piece_ref, p)) for p in z_peers]
    spread_x = [[go(remote(piece_ref, piece_ref, p)) for p in x_peers]]
    own_rows = pl.ds(pl.multiple_of(shard[0] * COLS, COLS), COLS)
    w_rows[0] = w_v[own_rows, :].reshape(8, 96, WIDTH)
    momentum_post(5)
    for i in range(3):
        spread_z[i].wait_recv()
        got = tot_out.at[c, x, zs[2 - i]]
        spread_x.append([go(remote(got, got, p)) for p in x_peers])
    quarter = tot_out.at[c, x]
    spread_core = [go(remote(quarter, quarter, sibling))]
    momentum_post(6)
    momentum_post(7)
    for copy in w_core + [act_l, act_r, act_o, act_fl, act_fr, act_fo]:
        copy.wait_recv()

    def input_grad(j, carry):
        rows = pl.ds(pl.multiple_of(j * 64, 64), 64)
        acc = jnp.zeros((64, COLS), F32)
        for s in range(8):
            acc = acc + lax.dot_general(
                act[s, rows, :], w_rows[s].reshape(COLS, WIDTH),
                (((1,), (1,)), ((), ())), preferred_element_type=F32,
            )
        grad_out[rows, :] = acc.astype(BF16)
        return carry

    lax.fori_loop(0, TOK // 64, input_grad, 0)

    for i in range(3):
        for copies in spread_x:
            copies[i].wait_recv()
        got = tot_out.at[c, xs[2 - i]]
        spread_core.append(go(remote(got, got, sibling)))
    for copy in spread_core:
        copy.wait_recv()
    for copy in outgoing:
        copy.wait_send()


def write_kernel(scale, grad_ref, mom_ref, total_ref, decoder_ref, grad_out, mom_out, upd_out, update, sems):
    x, y, zh, zl, c = position()
    zo = 1 - zh
    ys = (y, (y + 3) % 4, (y + 1) % 4, (y + 2) % 4)
    shard = [zh * 4 + v for v in ys] + [zo * 4 + v for v in ys]
    copies = []

    def put(src, dst):
        copies.append(pltpu.make_async_copy(src, dst, sems.at[len(copies)]))
        copies[-1].start()

    for s in range(8):
        rows = pl.ds(pl.multiple_of(shard[s] * COLS, COLS), COLS)
        put(mom_ref.at[pl.ds(s * COLS, COLS)], mom_out.at[0, rows])
    put(grad_ref, grad_out)
    for s in range(8):
        coded = total_ref[s // 4, s % 4].reshape(CODED, WIDTH)
        for j in range(COLS // CHUNK):
            update[pl.ds(s * COLS + j * CHUNK, CHUNK), :] = scale * jnp.dot(
                decoder_ref[...], coded[j * SPAN:(j + 1) * SPAN], preferred_element_type=F32
            )
        rows = pl.ds(pl.multiple_of(shard[s] * COLS, COLS), COLS)
        put(update.at[pl.ds(s * COLS, COLS)], upd_out.at[rows])
    for copy in copies:
        copy.wait()


def per_device(tokens, cotangent, weights, momentum):
    replicas = lax.axis_size("replica")
    coder_c = jnp.asarray(coder(), F32).astype(BF16)
    decoder_c = jnp.asarray(decoder(), F32).astype(BF16)
    vmem = pl.BlockSpec(memory_space=pltpu.VMEM)
    hbm = pl.BlockSpec(memory_space=pltpu.HBM)
    copies = 100
    input_grad, momentum_out, total = pl.pallas_call(
        step_kernel,
        out_shape=(
            pltpu.VMEM((TOK, COLS), BF16),
            pltpu.VMEM((D, WIDTH), F32),
            pltpu.VMEM((2, 4, 4, 48, WIDTH), BF16),
        ),
        in_specs=[hbm, vmem, hbm, hbm, vmem],
        out_specs=(vmem, vmem, vmem),
        scratch_shapes=[
            pltpu.VMEM((8, TOK, COLS), BF16),
            pltpu.VMEM((D, WIDTH), BF16),
            pltpu.VMEM((D, WIDTH), F32),
            pltpu.VMEM((D, TOK), BF16),
            pltpu.VMEM((8 * CODED, TOK), BF16),
            pltpu.VMEM((8 * CODED, WIDTH), F32),
            pltpu.VMEM((TOK, WIDTH), F32),
            pltpu.VMEM((8, TOK, WIDTH), BF16),
            pltpu.VMEM((8, 8, 96, WIDTH), BF16),
            pltpu.VMEM((4, CODED, WIDTH), BF16),
            pltpu.VMEM((4, CODED, WIDTH), BF16),
            pltpu.VMEM((3, CODED, WIDTH), BF16),
            pltpu.VMEM((CODED, WIDTH), F32),
            pltpu.VMEM((3, CODED, WIDTH), BF16),
            pltpu.VMEM((4, 48, WIDTH), F32),
            pltpu.VMEM((4, 48, WIDTH), BF16),
            pltpu.VMEM((3, 48, WIDTH), BF16),
            pltpu.SemaphoreType.DMA((copies,)),
            pltpu.SemaphoreType.DMA((copies,)),
            pltpu.SemaphoreType.DMA((3,)),
        ],
        compiler_params=pltpu.CompilerParams(
            collective_id=0, has_side_effects=True, vmem_limit_bytes=52 << 20
        ),
        name="step",
    )(tokens, cotangent, weights, momentum[0], coder_c)
    return pl.pallas_call(
        lambda *refs: write_kernel(1.0 / math.sqrt(replicas), *refs),
        out_shape=(
            jax.ShapeDtypeStruct((TOK, COLS), BF16),
            jax.ShapeDtypeStruct((1, D, WIDTH), F32),
            jax.ShapeDtypeStruct((D, WIDTH), F32),
        ),
        in_specs=[vmem] * 4,
        out_specs=(hbm, hbm, hbm),
        scratch_shapes=[pltpu.VMEM((D, WIDTH), F32), pltpu.SemaphoreType.DMA((17,))],
        compiler_params=pltpu.CompilerParams(vmem_limit_bytes=16 << 20),
        name="write",
    )(input_grad, momentum_out, total, decoder_c)


def solution(mesh):
    in_specs = (
        P("replica", "tensor"),
        P("replica", "tensor"),
        P(None, "tensor"),
        P("replica", None, "tensor"),
    )
    out_specs = (P("replica", "tensor"), P("replica", None, "tensor"), P(None, "tensor"))
    return jax.shard_map(
        per_device, mesh=mesh, in_specs=in_specs, out_specs=out_specs, check_vma=False
    )
```

```python
import math

import jax
import jax.numpy as jnp
import numpy as np
from jax import lax
from jax.experimental import pallas as pl
from jax.experimental.pallas import tpu as pltpu
from jax.sharding import PartitionSpec as P

SPAN = 64
KEEP = 16
D = 6144
TOK = 320
COLS = 768
WIDTH = 128
CODED = 192
CHUNK = 256
FIRST = 256
DECAY = 0.9
MESH = pl.DeviceIdType.MESH
F32 = jnp.float32
BF16 = jnp.bfloat16


def cosine_basis():
    order = np.arange(SPAN, dtype=np.float64)[:, None]
    place = np.arange(SPAN, dtype=np.float64)[None, :]
    table = np.cos(np.pi * (place + 0.5) * order / SPAN) * math.sqrt(2.0 / SPAN)
    return np.where(order == 0, table * math.sqrt(0.5), table)


def cosine_table():
    return cosine_basis()[:KEEP]


def shard_basis():
    blocks = np.kron(np.eye(COLS // SPAN), cosine_basis().T).reshape(COLS, COLS // SPAN, SPAN)
    kept = blocks[:, :, :KEEP].reshape(COLS, -1)
    others = blocks[:, :, KEEP:].reshape(COLS, -1)
    return np.concatenate([kept, others], axis=1)


def coder():
    table = cosine_table()
    four = np.eye(CHUNK // SPAN)
    rest = np.kron(four, np.eye(SPAN) - table.T @ table)
    return np.concatenate([rest, np.kron(four, table)], axis=0)


def decoder():
    return np.kron(np.eye(CHUNK // SPAN), cosine_table().T)


def position():
    t = lax.axis_index("tensor")
    r = lax.axis_index("replica")
    return r // 8, t % 4, t // 4, (r // 2) % 4, r % 2


def device(x, y, zh, zl, c):
    return (zh * 4 + y, (x * 4 + zl) * 2 + c)


def step_kernel(
    tok_h, cot_h, w_h, mom_h, coder_h, basis_h, rest_h, pick_h,
    grad_out, mom_out, tot_out,
    coder_ref, basis_ref, rest_ref, pick_ref, cot_ref,
    gathered, spectra_own, spectra, w_v, w_far, w_rows, mom_v, high_t, low_t, low_pre,
    hidden, hidden_far, give_far, take_far, act,
    to_core, from_core, part_x, kept_x, from_x, part_z, to_z, from_z,
    send, recv, local,
):
    x, y, zh, zl, c = position()
    yr, yl, yo = (y + 1) % 4, (y + 3) % 4, (y + 2) % 4
    zo = 1 - zh
    right, left, opp = device(x, yr, zh, zl, c), device(x, yl, zh, zl, c), device(x, yo, zh, zl, c)
    far = device(x, y, zo, zl, c)
    sibling = device(x, y, zh, zl, 1 - c)
    xs = [(x + d) % 4 for d in (1, 2, 3)]
    zs = [(zl + d) % 4 for d in (1, 2, 3)]
    x_peers = [device(v, y, zh, zl, c) for v in xs]
    z_peers = [device(x, y, zh, v, c) for v in zs]
    places = (y, yl, yr, yo)
    shard = [zh * 4 + v for v in places] + [zo * 4 + v for v in places]
    counter = iter(range(1000))

    def remote(src, dst, target):
        k = next(counter)
        return pltpu.make_async_remote_copy(
            src_ref=src, dst_ref=dst, send_sem=send.at[k], recv_sem=recv.at[k],
            device_id=target, device_id_type=MESH,
        )

    barrier = pltpu.get_barrier_semaphore()
    partners = [right, left, opp, far, sibling] + x_peers + z_peers
    for p in partners:
        pl.semaphore_signal(barrier, inc=1, device_id=p, device_id_type=MESH)

    def fetch(src, dst, k):
        copy = pltpu.make_async_copy(src, dst, local.at[k])
        copy.start()
        return copy

    tok_in = fetch(tok_h, gathered.at[0], 0)
    basis_in = fetch(basis_h, basis_ref, 1)
    coder_in = fetch(coder_h, coder_ref, 2)
    mom_in = fetch(mom_h, mom_v, 3)
    w_in = fetch(w_h, w_v, 4)
    rest_in = fetch(rest_h, rest_ref, 5)
    pick_in = fetch(pick_h, pick_ref, 6)
    cot_in = fetch(cot_h, cot_ref, 7)

    outgoing = []

    def go(copy):
        copy.start()
        outgoing.append(copy)
        return copy

    def spectrum(j):
        cols = slice(j * CHUNK, (j + 1) * CHUNK)
        spectra_own[:, cols] = jnp.dot(
            gathered[0], basis_ref[:, cols], preferred_element_type=F32
        ).astype(BF16)

    def code_tokens(slot):
        for j in range(COLS // CHUNK):
            coded = lax.dot_general(
                coder_ref[...], gathered[slot, :, j * CHUNK:(j + 1) * CHUNK],
                (((1,), (1,)), ((), ())), preferred_element_type=F32,
            ).astype(BF16)
            high_t[pl.ds(slot * COLS + j * CHUNK, CHUNK), :] = coded[:CHUNK]
            low_t[pl.ds(slot * CODED + j * SPAN, SPAN), :] = coded[CHUNK:]

    def low_far(i):
        low_t[pl.ds((4 + i) * CODED, CODED), :] = lax.dot_general(
            pick_ref[...], spectra[i, :, :FIRST],
            (((1,), (1,)), ((), ())), preferred_element_type=F32,
        ).astype(BF16)

    def high_far(i):
        for j in range(COLS // CHUNK):
            high_t[pl.ds((4 + i) * COLS + j * CHUNK, CHUNK), :] = lax.dot_general(
                rest_ref[j * CHUNK:(j + 1) * CHUNK, :], spectra[i],
                (((1,), (1,)), ((), ())), preferred_element_type=F32,
            ).astype(BF16)

    def add_hidden(slot):
        rows = gathered[slot]
        hidden[...] += jnp.dot(
            rows, w_v[shard[slot]].reshape(COLS, WIDTH), preferred_element_type=F32
        )
        hidden_far[...] += jnp.dot(
            rows, w_far[places[slot]].reshape(COLS, WIDTH), preferred_element_type=F32
        )

    def momentum_pre(slot):
        for j in range(COLS // CHUNK):
            rows = pl.ds(pl.multiple_of(shard[slot] * COLS + j * CHUNK, CHUNK), CHUNK)
            coded = DECAY * jnp.dot(
                coder_ref[...], mom_v[rows, :].astype(BF16), preferred_element_type=F32
            )
            mom_out[pl.ds(slot * COLS + j * CHUNK, CHUNK), :] = coded[:CHUNK]
            low_pre[pl.ds(slot * CODED + j * SPAN, SPAN), :] = coded[CHUNK:]

    hidden[...] = jnp.zeros_like(hidden)
    hidden_far[...] = jnp.zeros_like(hidden_far)
    tok_in.wait()
    basis_in.wait()
    for j in range(COLS // CHUNK):
        spectrum(j)

    pl.semaphore_wait(barrier, len(partners))

    half = TOK // 2
    first, second = pl.ds(0, half), pl.ds(half, half)
    piece = 64
    pieces = TOK // piece
    lows, highs = pl.ds(0, FIRST), pl.ds(FIRST, COLS - FIRST)

    w_z = go(remote(w_h.at[pl.ds(zo * 4, 4), x, c], w_far.at[:, x, c], far))
    from_l1 = go(remote(tok_h.at[first], gathered.at[1, first], right))
    from_r2 = go(remote(tok_h.at[second], gathered.at[2, second], left))
    from_l2 = go(remote(tok_h.at[second], gathered.at[1, second], right))
    from_r1 = go(remote(tok_h.at[first], gathered.at[2, first], left))
    coder_in.wait()
    code_tokens(0)
    mom_in.wait()
    for s in range(4):
        momentum_pre(s)
    low_z = go(remote(spectra_own.at[:, lows], spectra.at[0, :, lows], far))
    high_z, high_r, high_l, high_o = [], [], [], []

    def send_high():
        rows = pl.ds(len(high_z) * piece, piece)
        high_z.append(go(remote(spectra_own.at[rows, highs], spectra.at[0, rows, highs], far)))

    def forward_high(i):
        rows = pl.ds(i * piece, piece)
        high_z[i].wait_recv()
        high_r.append(go(remote(spectra.at[0, rows, highs], spectra.at[1, rows, highs], right)))
        high_l.append(go(remote(spectra.at[0, rows, highs], spectra.at[2, rows, highs], left)))

    def forward_high_opp(i):
        lower = pl.ds(i * piece, piece // 2)
        upper = pl.ds(i * piece + piece // 2, piece // 2)
        high_r[i].wait_recv()
        high_o.append(go(remote(spectra.at[1, lower, highs], spectra.at[3, lower, highs], right)))
        high_l[i].wait_recv()
        high_o.append(go(remote(spectra.at[2, upper, highs], spectra.at[3, upper, highs], left)))

    send_high()
    send_high()
    send_high()
    for s in range(4, 8):
        momentum_pre(s)
    w_z.wait_recv()
    w_x = [go(remote(w_far.at[:, x, c], w_far.at[:, x, c], p)) for p in x_peers]
    from_l1.wait_recv()
    opp1 = go(remote(gathered.at[1, first], gathered.at[3, first], right))
    from_r2.wait_recv()
    opp2 = go(remote(gathered.at[2, second], gathered.at[3, second], left))
    send_high()
    for copy in w_x:
        copy.wait_recv()
    w_core = go(remote(w_far.at[:, :, c], w_far.at[:, :, c], sibling))
    from_l2.wait_recv()
    code_tokens(1)
    from_r1.wait_recv()
    code_tokens(2)
    w_in.wait()
    w_core.wait_recv()
    add_hidden(0)
    add_hidden(1)
    add_hidden(2)
    opp1.wait_recv()
    opp2.wait_recv()
    low_z.wait_recv()
    low_r = go(remote(spectra.at[0, :, lows], spectra.at[1, :, lows], right))
    low_l = go(remote(spectra.at[0, :, lows], spectra.at[2, :, lows], left))
    add_hidden(3)
    give_far[...] = hidden_far[...].astype(BF16)
    hidden_z = go(remote(give_far, take_far, far))
    send_high()
    code_tokens(3)
    pick_in.wait()
    low_far(0)
    mirror = [0, 2, 1, 3]
    near = [None, left, right, opp]
    rows_y = []

    low_r.wait_recv()
    low_o1 = go(remote(spectra.at[1, first, lows], spectra.at[3, first, lows], right))
    low_l.wait_recv()
    low_o2 = go(remote(spectra.at[2, second, lows], spectra.at[3, second, lows], left))
    for s in range(1, 4):
        rows_y.append(
            go(remote(w_v.at[shard[s], x, c], w_rows.at[mirror[s] - 1, x, c], near[s]))
        )
        rows_y.append(
            go(remote(w_far.at[places[s], x, c], w_rows.at[mirror[s] + 2, x, c], near[s]))
        )
    low_far(1)
    low_far(2)
    cot_in.wait()
    hidden_z.wait_recv()

    h = hidden[...] + take_far[...].astype(F32)
    sig = jax.nn.sigmoid(h)
    act[0] = (cot_ref[...].astype(F32) * sig * (1.0 + h * (1.0 - sig))).astype(BF16)
    act_z = go(remote(act.at[0], act.at[4], far))

    inv = 1.0 / math.sqrt(TOK)

    def code(slot):
        rows = pl.ds(pl.multiple_of(slot * CODED, CODED), CODED)
        grad = jnp.dot(low_t[rows, :], act[0], preferred_element_type=F32)
        return low_pre[rows, :] + grad * inv

    def momentum_post(slot):
        rows = pl.ds(slot * COLS, COLS)
        grad = jnp.dot(high_t[rows, :], act[0], preferred_element_type=F32)
        mom_out[rows, :] = mom_out[rows, :] + grad * inv

    low_o1.wait_recv()
    low_o2.wait_recv()
    for i in range(4):
        forward_high(i)
    low_far(3)
    order = [xs[1], xs[0], xs[2], x]
    peers_of = [x_peers[1], x_peers[0], x_peers[2]]
    red_core = []
    for i, v in enumerate(order):
        to_core[i] = code((1 - c) * 4 + v).astype(BF16)
        red_core.append(go(remote(to_core.at[i], from_core.at[i], sibling)))
    red_x = []
    for i, v in enumerate(order):
        own = code(c * 4 + v)
        red_core[i].wait_recv()
        both = own + from_core[i].astype(F32)
        if i < 3:
            part_x[i] = both.astype(BF16)
            red_x.append(go(remote(part_x.at[i], from_x.at[i], peers_of[i])))
        else:
            kept_x[...] = both
    act_l = go(remote(act.at[0], act.at[1], right))
    act_r = go(remote(act.at[0], act.at[2], left))
    act_o = go(remote(act.at[0], act.at[3], opp))
    forward_high(4)
    for s in range(4):
        momentum_post(s)
    for copy in red_x:
        copy.wait_recv()
    part_z[...] = (
        kept_x[...] + from_x[0].astype(F32) + from_x[1].astype(F32) + from_x[2].astype(F32)
    ).reshape(4, 48, WIDTH)
    to_z[...] = part_z[...].astype(BF16)
    red_z = [
        go(remote(to_z.at[v], from_z.at[i], p)) for i, (v, p) in enumerate(zip(zs, z_peers))
    ]
    for copy in rows_y:
        copy.wait_recv()
    share = w_rows.at[:, x, c]
    rows_x = [go(remote(share, share, p)) for p in x_peers]
    act_z.wait_recv()
    act_fl = go(remote(act.at[4], act.at[5], right))
    act_fr = go(remote(act.at[4], act.at[6], left))
    act_fo = go(remote(act.at[4], act.at[7], opp))
    rest_in.wait()
    high_far(0)
    for copy in red_z:
        copy.wait_recv()
    tot_out[c, x, zl] = (
        part_z[zl] + from_z[0].astype(F32) + from_z[1].astype(F32) + from_z[2].astype(F32)
    ).astype(BF16)
    piece_ref = tot_out.at[c, x, zl]
    spread_z = [go(remote(piece_ref, piece_ref, p)) for p in z_peers]
    spread_x = [[go(remote(piece_ref, piece_ref, p)) for p in x_peers]]
    momentum_post(4)
    for i in range(2):
        forward_high_opp(i)
    for i in range(3):
        spread_z[i].wait_recv()
        got = tot_out.at[c, x, zs[2 - i]]
        spread_x.append([go(remote(got, got, p)) for p in x_peers])
    quarter = tot_out.at[c, x]
    spread_core = [go(remote(quarter, quarter, sibling))]
    for i in range(2, 5):
        forward_high_opp(i)
    for copy in rows_x:
        copy.wait_recv()
    rows_core = go(remote(w_rows.at[:, :, c], w_rows.at[:, :, c], sibling))
    high_far(1)
    momentum_post(5)
    for i in range(3):
        for copies in spread_x:
            copies[i].wait_recv()
        got = tot_out.at[c, xs[2 - i]]
        spread_core.append(go(remote(got, got, sibling)))
    high_far(2)
    momentum_post(6)
    for copy in high_o:
        copy.wait_recv()
    high_far(3)
    momentum_post(7)
    for copy in [rows_core, act_l, act_r, act_o, act_fl, act_fr, act_fo]:
        copy.wait_recv()

    def weight_rows(s):
        if s == 0:
            return w_v[shard[0]].reshape(COLS, WIDTH)
        if s == 4:
            return w_far[y].reshape(COLS, WIDTH)
        return w_rows[s - 1 if s < 4 else s - 2].reshape(COLS, WIDTH)

    for j in range(COLS // CHUNK):
        cols = slice(j * CHUNK, (j + 1) * CHUNK)
        acc = jnp.zeros((TOK, CHUNK), F32)
        for s in range(8):
            acc = acc + lax.dot_general(
                act[s], weight_rows(s)[cols], (((1,), (1,)), ((), ())),
                preferred_element_type=F32,
            )
        grad_out[:, cols] = acc.astype(BF16)

    for copy in spread_core:
        copy.wait_recv()
    for copy in outgoing:
        copy.wait_send()


def write_kernel(scale, grad_ref, mom_ref, total_ref, decoder_ref, grad_out, mom_out, upd_out, update, sems):
    x, y, zh, zl, c = position()
    zo = 1 - zh
    ys = (y, (y + 3) % 4, (y + 1) % 4, (y + 2) % 4)
    shard = [zh * 4 + v for v in ys] + [zo * 4 + v for v in ys]
    copies = []

    def put(src, dst):
        copies.append(pltpu.make_async_copy(src, dst, sems.at[len(copies)]))
        copies[-1].start()

    for s in range(8):
        rows = pl.ds(pl.multiple_of(shard[s] * COLS, COLS), COLS)
        put(mom_ref.at[pl.ds(s * COLS, COLS)], mom_out.at[0, rows])
    put(grad_ref, grad_out)
    for s in range(8):
        coded = total_ref[s // 4, s % 4].reshape(CODED, WIDTH)
        for j in range(COLS // CHUNK):
            update[pl.ds(s * COLS + j * CHUNK, CHUNK), :] = scale * jnp.dot(
                decoder_ref[...], coded[j * SPAN:(j + 1) * SPAN], preferred_element_type=F32
            )
        rows = pl.ds(pl.multiple_of(shard[s] * COLS, COLS), COLS)
        put(update.at[pl.ds(s * COLS, COLS)], upd_out.at[rows])
    for copy in copies:
        copy.wait()


def per_device(tokens, cotangent, weights, momentum):
    replicas = lax.axis_size("replica")

    def constant(values):
        return jnp.asarray(values, F32).astype(BF16)

    basis = shard_basis()
    rest = np.where(np.arange(COLS)[None, :] < CODED, 0.0, basis)
    pick = np.eye(CODED, FIRST)
    decoder_c = constant(decoder())
    vmem = pl.BlockSpec(memory_space=pltpu.VMEM)
    hbm = pl.BlockSpec(memory_space=pltpu.HBM)
    copies = 120
    split = (4, 2, 96, WIDTH)
    input_grad, momentum_out, total = pl.pallas_call(
        step_kernel,
        out_shape=(
            pltpu.VMEM((TOK, COLS), BF16),
            pltpu.VMEM((D, WIDTH), F32),
            pltpu.VMEM((2, 4, 4, 48, WIDTH), BF16),
        ),
        in_specs=[hbm] * 8,
        out_specs=(vmem, vmem, vmem),
        scratch_shapes=[
            pltpu.VMEM((CHUNK + SPAN, CHUNK), BF16),
            pltpu.VMEM((COLS, COLS), BF16),
            pltpu.VMEM((COLS, COLS), BF16),
            pltpu.VMEM((CODED, FIRST), BF16),
            pltpu.VMEM((TOK, WIDTH), BF16),
            pltpu.VMEM((4, TOK, COLS), BF16),
            pltpu.VMEM((TOK, COLS), BF16),
            pltpu.VMEM((4, TOK, COLS), BF16),
            pltpu.VMEM((8,) + split, BF16),
            pltpu.VMEM((4,) + split, BF16),
            pltpu.VMEM((6,) + split, BF16),
            pltpu.VMEM((D, WIDTH), F32),
            pltpu.VMEM((D, TOK), BF16),
            pltpu.VMEM((8 * CODED, TOK), BF16),
            pltpu.VMEM((8 * CODED, WIDTH), F32),
            pltpu.VMEM((TOK, WIDTH), F32),
            pltpu.VMEM((TOK, WIDTH), F32),
            pltpu.VMEM((TOK, WIDTH), BF16),
            pltpu.VMEM((TOK, WIDTH), BF16),
            pltpu.VMEM((8, TOK, WIDTH), BF16),
            pltpu.VMEM((4, CODED, WIDTH), BF16),
            pltpu.VMEM((4, CODED, WIDTH), BF16),
            pltpu.VMEM((3, CODED, WIDTH), BF16),
            pltpu.VMEM((CODED, WIDTH), F32),
            pltpu.VMEM((3, CODED, WIDTH), BF16),
            pltpu.VMEM((4, 48, WIDTH), F32),
            pltpu.VMEM((4, 48, WIDTH), BF16),
            pltpu.VMEM((3, 48, WIDTH), BF16),
            pltpu.SemaphoreType.DMA((copies,)),
            pltpu.SemaphoreType.DMA((copies,)),
            pltpu.SemaphoreType.DMA((8,)),
        ],
        compiler_params=pltpu.CompilerParams(
            collective_id=0, has_side_effects=True, vmem_limit_bytes=52 << 20
        ),
        name="step",
    )(
        tokens, cotangent, weights.reshape((8,) + split), momentum[0],
        constant(coder()), constant(basis), constant(rest), constant(pick),
    )
    return pl.pallas_call(
        lambda *refs: write_kernel(1.0 / math.sqrt(replicas), *refs),
        out_shape=(
            jax.ShapeDtypeStruct((TOK, COLS), BF16),
            jax.ShapeDtypeStruct((1, D, WIDTH), F32),
            jax.ShapeDtypeStruct((D, WIDTH), F32),
        ),
        in_specs=[vmem] * 4,
        out_specs=(hbm, hbm, hbm),
        scratch_shapes=[pltpu.VMEM((D, WIDTH), F32), pltpu.SemaphoreType.DMA((17,))],
        compiler_params=pltpu.CompilerParams(vmem_limit_bytes=16 << 20),
        name="write",
    )(input_grad, momentum_out, total, decoder_c)


def solution(mesh):
    in_specs = (
        P("replica", "tensor"),
        P("replica", "tensor"),
        P(None, "tensor"),
        P("replica", None, "tensor"),
    )
    out_specs = (P("replica", "tensor"), P("replica", None, "tensor"), P(None, "tensor"))
    return jax.shard_map(
        per_device, mesh=mesh, in_specs=in_specs, out_specs=out_specs, check_vma=False
    )
```

```python
import math

import jax
import jax.numpy as jnp
import numpy as np
from jax import lax
from jax.experimental import pallas as pl
from jax.experimental.pallas import tpu as pltpu
from jax.sharding import PartitionSpec as P

SPAN = 64
KEEP = 16
D = 6144
TOK = 320
COLS = 768
WIDTH = 128
CODED = 192
CHUNK = 256
FIRST = 256
DECAY = 0.9
MESH = pl.DeviceIdType.MESH
F32 = jnp.float32
BF16 = jnp.bfloat16


def cosine_basis():
    order = np.arange(SPAN, dtype=np.float64)[:, None]
    place = np.arange(SPAN, dtype=np.float64)[None, :]
    table = np.cos(np.pi * (place + 0.5) * order / SPAN) * math.sqrt(2.0 / SPAN)
    return np.where(order == 0, table * math.sqrt(0.5), table)


def cosine_table():
    return cosine_basis()[:KEEP]


def shard_basis():
    blocks = np.kron(np.eye(COLS // SPAN), cosine_basis().T).reshape(COLS, COLS // SPAN, SPAN)
    kept = blocks[:, :, :KEEP].reshape(COLS, -1)
    others = blocks[:, :, KEEP:].reshape(COLS, -1)
    return np.concatenate([kept, others], axis=1)


def coder():
    table = cosine_table()
    four = np.eye(CHUNK // SPAN)
    rest = np.kron(four, np.eye(SPAN) - table.T @ table)
    return np.concatenate([rest, np.kron(four, table)], axis=0)


def decoder():
    return np.kron(np.eye(CHUNK // SPAN), cosine_table().T)


def position():
    t = lax.axis_index("tensor")
    r = lax.axis_index("replica")
    return r // 8, t % 4, t // 4, (r // 2) % 4, r % 2


def device(x, y, zh, zl, c):
    return (zh * 4 + y, (x * 4 + zl) * 2 + c)


def step_kernel(
    tok_h, cot_h, w_h, mom_h, coder_h, basis_h, rest_h, pick_h,
    grad_out, mom_out, tot_out,
    coder_ref, basis_ref, rest_ref, pick_ref, cot_ref,
    gathered, spectra_own, spectra, w_pair, w_rows, mom_v, high_t, low_t, low_pre,
    hidden, give_far, take_far, act,
    to_core, from_core, part_x, kept_x, from_x, part_z, to_z, from_z,
    send, recv, local,
):
    x, y, zh, zl, c = position()
    yr, yl, yo = (y + 1) % 4, (y + 3) % 4, (y + 2) % 4
    zo = 1 - zh
    right, left, opp = device(x, yr, zh, zl, c), device(x, yl, zh, zl, c), device(x, yo, zh, zl, c)
    far = device(x, y, zo, zl, c)
    sibling = device(x, y, zh, zl, 1 - c)
    xs = [(x + d) % 4 for d in (1, 2, 3)]
    zs = [(zl + d) % 4 for d in (1, 2, 3)]
    x_peers = [device(v, y, zh, zl, c) for v in xs]
    z_peers = [device(x, y, zh, v, c) for v in zs]
    places = (y, yl, yr, yo)
    shard = [zh * 4 + v for v in places] + [zo * 4 + v for v in places]
    counter = iter(range(1000))

    def remote(src, dst, target):
        k = next(counter)
        return pltpu.make_async_remote_copy(
            src_ref=src, dst_ref=dst, send_sem=send.at[k], recv_sem=recv.at[k],
            device_id=target, device_id_type=MESH,
        )

    barrier = pltpu.get_barrier_semaphore()
    partners = [right, left, opp, far, sibling] + x_peers + z_peers
    for p in partners:
        pl.semaphore_signal(barrier, inc=1, device_id=p, device_id_type=MESH)

    def fetch(src, dst, k):
        copy = pltpu.make_async_copy(src, dst, local.at[k])
        copy.start()
        return copy

    tok_in = fetch(tok_h, gathered.at[0], 0)
    basis_in = fetch(basis_h, basis_ref, 1)
    coder_in = fetch(coder_h, coder_ref, 2)
    mom_in = fetch(mom_h, mom_v, 3)
    nears, fars = pl.ds(0, WIDTH), pl.ds(WIDTH, WIDTH)
    w_in = fetch(w_h.at[pl.ds(zh * 4, 4)], w_pair.at[:, :, :, :, nears], 4)
    rest_in = fetch(rest_h, rest_ref, 5)
    pick_in = fetch(pick_h, pick_ref, 6)
    cot_in = fetch(cot_h, cot_ref, 7)

    outgoing = []

    def go(copy):
        copy.start()
        outgoing.append(copy)
        return copy

    def spectrum(j):
        cols = slice(j * CHUNK, (j + 1) * CHUNK)
        spectra_own[:, cols] = jnp.dot(
            gathered[0], basis_ref[:, cols], preferred_element_type=F32
        ).astype(BF16)

    def code_tokens(slot):
        for j in range(COLS // CHUNK):
            coded = lax.dot_general(
                coder_ref[...], gathered[slot, :, j * CHUNK:(j + 1) * CHUNK],
                (((1,), (1,)), ((), ())), preferred_element_type=F32,
            ).astype(BF16)
            high_t[pl.ds(slot * COLS + j * CHUNK, CHUNK), :] = coded[:CHUNK]
            low_t[pl.ds(slot * CODED + j * SPAN, SPAN), :] = coded[CHUNK:]

    def low_far(i):
        low_t[pl.ds((4 + i) * CODED, CODED), :] = lax.dot_general(
            pick_ref[...], spectra[i, :, :FIRST],
            (((1,), (1,)), ((), ())), preferred_element_type=F32,
        ).astype(BF16)

    def high_far(i):
        for j in range(COLS // CHUNK):
            high_t[pl.ds((4 + i) * COLS + j * CHUNK, CHUNK), :] = lax.dot_general(
                rest_ref[j * CHUNK:(j + 1) * CHUNK, :], spectra[i],
                (((1,), (1,)), ((), ())), preferred_element_type=F32,
            ).astype(BF16)

    def add_hidden(slot, rows):
        hidden[rows, :] += jnp.dot(
            gathered[slot, rows, :], w_pair[places[slot]].reshape(COLS, 2 * WIDTH),
            preferred_element_type=F32,
        )

    def momentum_pre(slot):
        for j in range(COLS // CHUNK):
            rows = pl.ds(pl.multiple_of(shard[slot] * COLS + j * CHUNK, CHUNK), CHUNK)
            coded = DECAY * jnp.dot(
                coder_ref[...], mom_v[rows, :].astype(BF16), preferred_element_type=F32
            )
            mom_out[pl.ds(slot * COLS + j * CHUNK, CHUNK), :] = coded[:CHUNK]
            low_pre[pl.ds(slot * CODED + j * SPAN, SPAN), :] = coded[CHUNK:]

    hidden[...] = jnp.zeros_like(hidden)
    tok_in.wait()
    basis_in.wait()
    for j in range(COLS // CHUNK):
        spectrum(j)

    pl.semaphore_wait(barrier, len(partners))

    half = TOK // 2
    halves = [pl.ds(0, half), pl.ds(half, half)]
    upper = [pl.ds(0, half // 2), pl.ds(half, half // 2)]
    lower = [pl.ds(half // 2, half // 2), pl.ds(half + half // 2, half // 2)]
    piece = 64
    pieces = TOK // piece
    lows, highs = pl.ds(0, FIRST), pl.ds(FIRST, COLS - FIRST)

    w_z = go(remote(w_h.at[pl.ds(zo * 4, 4), x, c], w_pair.at[:, x, c, :, fars], far))
    from_l = [go(remote(tok_h.at[halves[0]], gathered.at[1, halves[0]], right))]
    from_r = [go(remote(tok_h.at[halves[0]], gathered.at[2, halves[0]], left))]
    coder_in.wait()
    code_tokens(0)
    mom_in.wait()
    for s in range(4):
        momentum_pre(s)
    low_z = go(remote(spectra_own.at[:, lows], spectra.at[0, :, lows], far))
    high_z, high_r, high_l, high_o = [], [], [], []

    def send_high():
        rows = pl.ds(len(high_z) * piece, piece)
        high_z.append(go(remote(spectra_own.at[rows, highs], spectra.at[0, rows, highs], far)))

    def forward_high(i):
        rows = pl.ds(i * piece, piece)
        high_z[i].wait_recv()
        high_r.append(go(remote(spectra.at[0, rows, highs], spectra.at[1, rows, highs], right)))
        high_l.append(go(remote(spectra.at[0, rows, highs], spectra.at[2, rows, highs], left)))

    def forward_high_opp(i):
        one = pl.ds(i * piece, piece // 2)
        two = pl.ds(i * piece + piece // 2, piece // 2)
        high_r[i].wait_recv()
        high_o.append(go(remote(spectra.at[1, one, highs], spectra.at[3, one, highs], right)))
        high_l[i].wait_recv()
        high_o.append(go(remote(spectra.at[2, two, highs], spectra.at[3, two, highs], left)))

    send_high()
    for s in range(4, 8):
        momentum_pre(s)
    from_l.append(go(remote(tok_h.at[halves[1]], gathered.at[1, halves[1]], right)))
    from_r.append(go(remote(tok_h.at[halves[1]], gathered.at[2, halves[1]], left)))
    w_z.wait_recv()
    share = w_pair.at[:, x, c, :, fars]
    w_x = [go(remote(share, share, p)) for p in x_peers]
    from_o = []

    def forward_tokens(i):
        from_l[i].wait_recv()
        from_o.append(go(remote(gathered.at[1, upper[i]], gathered.at[3, upper[i]], right)))
        from_r[i].wait_recv()
        from_o.append(go(remote(gathered.at[2, lower[i]], gathered.at[3, lower[i]], left)))

    forward_tokens(0)
    send_high()
    send_high()
    for copy in w_x:
        copy.wait_recv()
    share = w_pair.at[:, :, c, :, fars]
    w_core = go(remote(share, share, sibling))
    forward_tokens(1)
    code_tokens(1)
    code_tokens(2)
    w_in.wait()
    w_core.wait_recv()
    for s in range(3):
        add_hidden(s, halves[0])
    from_o[0].wait_recv()
    from_o[1].wait_recv()
    add_hidden(3, halves[0])
    hidden_z = []

    def send_hidden(i):
        give_far[halves[i], :] = hidden[halves[i], fars].astype(BF16)
        hidden_z.append(go(remote(give_far.at[halves[i]], take_far.at[halves[i]], far)))

    send_hidden(0)
    for s in range(3):
        add_hidden(s, halves[1])
    low_z.wait_recv()
    from_o[2].wait_recv()
    from_o[3].wait_recv()
    low_r = [go(remote(spectra.at[0, halves[0], lows], spectra.at[1, halves[0], lows], right))]
    low_l = [go(remote(spectra.at[0, halves[0], lows], spectra.at[2, halves[0], lows], left))]
    add_hidden(3, halves[1])
    send_hidden(1)
    low_r.append(go(remote(spectra.at[0, halves[1], lows], spectra.at[1, halves[1], lows], right)))
    low_l.append(go(remote(spectra.at[0, halves[1], lows], spectra.at[2, halves[1], lows], left)))
    send_high()
    send_high()
    code_tokens(3)
    pick_in.wait()
    low_far(0)
    low_o = []
    for i in range(2):
        low_r[i].wait_recv()
        low_o.append(go(remote(spectra.at[1, upper[i], lows], spectra.at[3, upper[i], lows], right)))
        low_l[i].wait_recv()
        low_o.append(go(remote(spectra.at[2, lower[i], lows], spectra.at[3, lower[i], lows], left)))
    mirror = [0, 2, 1, 3]
    near = [None, left, right, opp]
    rows_y = [
        go(remote(w_pair.at[places[s], x, c], w_rows.at[mirror[s] - 1, x, c], near[s]))
        for s in range(1, 4)
    ]
    low_far(1)
    low_far(2)
    cot_in.wait()
    for copy in hidden_z:
        copy.wait_recv()

    h = hidden[:, nears] + take_far[...].astype(F32)
    sig = jax.nn.sigmoid(h)
    act[0, :, nears] = (cot_ref[...].astype(F32) * sig * (1.0 + h * (1.0 - sig))).astype(BF16)
    act_z = go(remote(act.at[0, :, nears], act.at[0, :, fars], far))

    inv = 1.0 / math.sqrt(TOK)

    def code(slot):
        rows = pl.ds(pl.multiple_of(slot * CODED, CODED), CODED)
        grad = jnp.dot(low_t[rows, :], act[0, :, nears], preferred_element_type=F32)
        return low_pre[rows, :] + grad * inv

    def momentum_post(slot):
        rows = pl.ds(slot * COLS, COLS)
        grad = jnp.dot(high_t[rows, :], act[0, :, nears], preferred_element_type=F32)
        mom_out[rows, :] = mom_out[rows, :] + grad * inv

    for copy in low_o:
        copy.wait_recv()
    for i in range(3):
        forward_high(i)
    low_far(3)
    order = [xs[1], xs[0], xs[2], x]
    peers_of = [x_peers[1], x_peers[0], x_peers[2]]
    red_core = []
    for i, v in enumerate(order):
        to_core[i] = code((1 - c) * 4 + v).astype(BF16)
        red_core.append(go(remote(to_core.at[i], from_core.at[i], sibling)))
    red_x = []
    for i, v in enumerate(order):
        own = code(c * 4 + v)
        red_core[i].wait_recv()
        both = own + from_core[i].astype(F32)
        if i < 3:
            part_x[i] = both.astype(BF16)
            red_x.append(go(remote(part_x.at[i], from_x.at[i], peers_of[i])))
        else:
            kept_x[...] = both
    act_l = go(remote(act.at[0, :, nears], act.at[1, :, nears], right))
    act_r = go(remote(act.at[0, :, nears], act.at[2, :, nears], left))
    act_o = go(remote(act.at[0, :, nears], act.at[3, :, nears], opp))
    for s in range(4):
        momentum_post(s)
    forward_high(3)
    for copy in red_x:
        copy.wait_recv()
    part_z[...] = (
        kept_x[...] + from_x[0].astype(F32) + from_x[1].astype(F32) + from_x[2].astype(F32)
    ).reshape(4, 48, WIDTH)
    to_z[...] = part_z[...].astype(BF16)
    red_z = [
        go(remote(to_z.at[v], from_z.at[i], p)) for i, (v, p) in enumerate(zip(zs, z_peers))
    ]
    for copy in rows_y:
        copy.wait_recv()
    share = w_rows.at[:, x, c]
    rows_x = [go(remote(share, share, p)) for p in x_peers]
    forward_high(4)
    act_z.wait_recv()
    act_fl = go(remote(act.at[0, :, fars], act.at[1, :, fars], right))
    act_fr = go(remote(act.at[0, :, fars], act.at[2, :, fars], left))
    act_fo = go(remote(act.at[0, :, fars], act.at[3, :, fars], opp))
    rest_in.wait()
    high_far(0)
    for copy in red_z:
        copy.wait_recv()
    tot_out[c, x, zl] = (
        part_z[zl] + from_z[0].astype(F32) + from_z[1].astype(F32) + from_z[2].astype(F32)
    ).astype(BF16)
    piece_ref = tot_out.at[c, x, zl]
    spread_z = [go(remote(piece_ref, piece_ref, p)) for p in z_peers]
    spread_x = [[go(remote(piece_ref, piece_ref, p)) for p in x_peers]]
    momentum_post(4)
    for i in range(2):
        forward_high_opp(i)
    for i in range(3):
        spread_z[i].wait_recv()
        got = tot_out.at[c, x, zs[2 - i]]
        spread_x.append([go(remote(got, got, p)) for p in x_peers])
    quarter = tot_out.at[c, x]
    spread_core = [go(remote(quarter, quarter, sibling))]
    for i in range(2, 5):
        forward_high_opp(i)
    for copy in rows_x:
        copy.wait_recv()
    rows_core = go(remote(w_rows.at[:, :, c], w_rows.at[:, :, c], sibling))
    high_far(1)
    momentum_post(5)
    for i in range(3):
        for copies in spread_x:
            copies[i].wait_recv()
        got = tot_out.at[c, xs[2 - i]]
        spread_core.append(go(remote(got, got, sibling)))
    high_far(2)
    momentum_post(6)
    for copy in high_o:
        copy.wait_recv()
    high_far(3)
    momentum_post(7)
    for copy in [rows_core, act_l, act_r, act_o, act_fl, act_fr, act_fo]:
        copy.wait_recv()

    def weight_rows(s):
        block = w_pair[y] if s == 0 else w_rows[s - 1]
        return block.reshape(COLS, 2 * WIDTH)

    for j in range(COLS // CHUNK):
        cols = slice(j * CHUNK, (j + 1) * CHUNK)
        acc = jnp.zeros((TOK, CHUNK), F32)
        for s in range(4):
            acc = acc + lax.dot_general(
                act[s], weight_rows(s)[cols], (((1,), (1,)), ((), ())),
                preferred_element_type=F32,
            )
        grad_out[:, cols] = acc.astype(BF16)

    for copy in spread_core:
        copy.wait_recv()
    for copy in outgoing:
        copy.wait_send()


def write_kernel(scale, grad_ref, mom_ref, total_ref, decoder_ref, grad_out, mom_out, upd_out, update, sems):
    x, y, zh, zl, c = position()
    zo = 1 - zh
    ys = (y, (y + 3) % 4, (y + 1) % 4, (y + 2) % 4)
    shard = [zh * 4 + v for v in ys] + [zo * 4 + v for v in ys]
    copies = []

    def put(src, dst):
        copies.append(pltpu.make_async_copy(src, dst, sems.at[len(copies)]))
        copies[-1].start()

    for s in range(8):
        rows = pl.ds(pl.multiple_of(shard[s] * COLS, COLS), COLS)
        put(mom_ref.at[pl.ds(s * COLS, COLS)], mom_out.at[0, rows])
    put(grad_ref, grad_out)
    for s in range(8):
        coded = total_ref[s // 4, s % 4].reshape(CODED, WIDTH)
        for j in range(COLS // CHUNK):
            update[pl.ds(s * COLS + j * CHUNK, CHUNK), :] = scale * jnp.dot(
                decoder_ref[...], coded[j * SPAN:(j + 1) * SPAN], preferred_element_type=F32
            )
        rows = pl.ds(pl.multiple_of(shard[s] * COLS, COLS), COLS)
        put(update.at[pl.ds(s * COLS, COLS)], upd_out.at[rows])
    for copy in copies:
        copy.wait()


def per_device(tokens, cotangent, weights, momentum):
    replicas = lax.axis_size("replica")

    def constant(values):
        return jnp.asarray(values, F32).astype(BF16)

    basis = shard_basis()
    rest = np.where(np.arange(COLS)[None, :] < CODED, 0.0, basis)
    pick = np.eye(CODED, FIRST)
    decoder_c = constant(decoder())
    vmem = pl.BlockSpec(memory_space=pltpu.VMEM)
    hbm = pl.BlockSpec(memory_space=pltpu.HBM)
    copies = 120
    split = (4, 2, 96, WIDTH)
    pair = (4, 2, 96, 2 * WIDTH)
    input_grad, momentum_out, total = pl.pallas_call(
        step_kernel,
        out_shape=(
            pltpu.VMEM((TOK, COLS), BF16),
            pltpu.VMEM((D, WIDTH), F32),
            pltpu.VMEM((2, 4, 4, 48, WIDTH), BF16),
        ),
        in_specs=[hbm] * 8,
        out_specs=(vmem, vmem, vmem),
        scratch_shapes=[
            pltpu.VMEM((CHUNK + SPAN, CHUNK), BF16),
            pltpu.VMEM((COLS, COLS), BF16),
            pltpu.VMEM((COLS, COLS), BF16),
            pltpu.VMEM((CODED, FIRST), BF16),
            pltpu.VMEM((TOK, WIDTH), BF16),
            pltpu.VMEM((4, TOK, COLS), BF16),
            pltpu.VMEM((TOK, COLS), BF16),
            pltpu.VMEM((4, TOK, COLS), BF16),
            pltpu.VMEM((4,) + pair, BF16),
            pltpu.VMEM((3,) + pair, BF16),
            pltpu.VMEM((D, WIDTH), F32),
            pltpu.VMEM((D, TOK), BF16),
            pltpu.VMEM((8 * CODED, TOK), BF16),
            pltpu.VMEM((8 * CODED, WIDTH), F32),
            pltpu.VMEM((TOK, 2 * WIDTH), F32),
            pltpu.VMEM((TOK, WIDTH), BF16),
            pltpu.VMEM((TOK, WIDTH), BF16),
            pltpu.VMEM((4, TOK, 2 * WIDTH), BF16),
            pltpu.VMEM((4, CODED, WIDTH), BF16),
            pltpu.VMEM((4, CODED, WIDTH), BF16),
            pltpu.VMEM((3, CODED, WIDTH), BF16),
            pltpu.VMEM((CODED, WIDTH), F32),
            pltpu.VMEM((3, CODED, WIDTH), BF16),
            pltpu.VMEM((4, 48, WIDTH), F32),
            pltpu.VMEM((4, 48, WIDTH), BF16),
            pltpu.VMEM((3, 48, WIDTH), BF16),
            pltpu.SemaphoreType.DMA((copies,)),
            pltpu.SemaphoreType.DMA((copies,)),
            pltpu.SemaphoreType.DMA((8,)),
        ],
        compiler_params=pltpu.CompilerParams(
            collective_id=0, has_side_effects=True, vmem_limit_bytes=52 << 20
        ),
        name="step",
    )(
        tokens, cotangent, weights.reshape((8,) + split), momentum[0],
        constant(coder()), constant(basis), constant(rest), constant(pick),
    )
    return pl.pallas_call(
        lambda *refs: write_kernel(1.0 / math.sqrt(replicas), *refs),
        out_shape=(
            jax.ShapeDtypeStruct((TOK, COLS), BF16),
            jax.ShapeDtypeStruct((1, D, WIDTH), F32),
            jax.ShapeDtypeStruct((D, WIDTH), F32),
        ),
        in_specs=[vmem] * 4,
        out_specs=(hbm, hbm, hbm),
        scratch_shapes=[pltpu.VMEM((D, WIDTH), F32), pltpu.SemaphoreType.DMA((17,))],
        compiler_params=pltpu.CompilerParams(vmem_limit_bytes=16 << 20),
        name="write",
    )(input_grad, momentum_out, total, decoder_c)


def solution(mesh):
    in_specs = (
        P("replica", "tensor"),
        P("replica", "tensor"),
        P(None, "tensor"),
        P("replica", None, "tensor"),
    )
    out_specs = (P("replica", "tensor"), P("replica", None, "tensor"), P(None, "tensor"))
    return jax.shard_map(
        per_device, mesh=mesh, in_specs=in_specs, out_specs=out_specs, check_vma=False
    )
```

```python
import math

import jax
import jax.numpy as jnp
import numpy as np
from jax import lax
from jax.experimental import pallas as pl
from jax.experimental.pallas import tpu as pltpu
from jax.sharding import PartitionSpec as P

SPAN = 64
KEEP = 16
D = 6144
TOK = 320
COLS = 768
WIDTH = 128
CODED = 192
CHUNK = 256
FIRST = 256
DECAY = 0.9
MESH = pl.DeviceIdType.MESH
F32 = jnp.float32
BF16 = jnp.bfloat16


def cosine_basis():
    order = np.arange(SPAN, dtype=np.float64)[:, None]
    place = np.arange(SPAN, dtype=np.float64)[None, :]
    table = np.cos(np.pi * (place + 0.5) * order / SPAN) * math.sqrt(2.0 / SPAN)
    return np.where(order == 0, table * math.sqrt(0.5), table)


def cosine_table():
    return cosine_basis()[:KEEP]


def shard_basis():
    blocks = np.kron(np.eye(COLS // SPAN), cosine_basis().T).reshape(COLS, COLS // SPAN, SPAN)
    kept = blocks[:, :, :KEEP].reshape(COLS, -1)
    others = blocks[:, :, KEEP:].reshape(COLS, -1)
    return np.concatenate([kept, others], axis=1)


def coder():
    table = cosine_table()
    four = np.eye(CHUNK // SPAN)
    rest = np.kron(four, np.eye(SPAN) - table.T @ table)
    return np.concatenate([rest, np.kron(four, table)], axis=0)


def decoder():
    return np.kron(np.eye(CHUNK // SPAN), cosine_table().T)


def position():
    t = lax.axis_index("tensor")
    r = lax.axis_index("replica")
    return r // 8, t % 4, t // 4, (r // 2) % 4, r % 2


def device(x, y, zh, zl, c):
    return (zh * 4 + y, (x * 4 + zl) * 2 + c)


def step_kernel(
    tok_h, cot_h, w_h, mom_h, coder_h, basis_h, rest_h, pick_h,
    grad_out, mom_out, tot_out,
    coder_ref, basis_ref, rest_ref, pick_ref, cot_ref,
    gathered, spectra_own, spectra, w_pair, w_rows, mom_v, high_t, low_t, low_pre,
    hidden, give_far, take_far, act,
    to_core, from_core, part_x, kept_x, from_x, part_z, to_z, from_z,
    send, recv, local,
):
    x, y, zh, zl, c = position()
    yr, yl, yo = (y + 1) % 4, (y + 3) % 4, (y + 2) % 4
    zo = 1 - zh
    right, left, opp = device(x, yr, zh, zl, c), device(x, yl, zh, zl, c), device(x, yo, zh, zl, c)
    far = device(x, y, zo, zl, c)
    sibling = device(x, y, zh, zl, 1 - c)
    xs = [(x + d) % 4 for d in (1, 2, 3)]
    zs = [(zl + d) % 4 for d in (1, 2, 3)]
    x_peers = [device(v, y, zh, zl, c) for v in xs]
    z_peers = [device(x, y, zh, v, c) for v in zs]
    places = (y, yl, yr, yo)
    shard = [zh * 4 + v for v in places] + [zo * 4 + v for v in places]
    counter = iter(range(1000))

    def remote(src, dst, target):
        k = next(counter)
        return pltpu.make_async_remote_copy(
            src_ref=src, dst_ref=dst, send_sem=send.at[k], recv_sem=recv.at[k],
            device_id=target, device_id_type=MESH,
        )

    barrier = pltpu.get_barrier_semaphore()
    partners = [right, left, opp, far, sibling] + x_peers + z_peers
    for p in partners:
        pl.semaphore_signal(barrier, inc=1, device_id=p, device_id_type=MESH)

    def fetch(src, dst, k):
        copy = pltpu.make_async_copy(src, dst, local.at[k])
        copy.start()
        return copy

    tok_in = fetch(tok_h, gathered.at[0], 0)
    basis_in = fetch(basis_h, basis_ref, 1)
    coder_in = fetch(coder_h, coder_ref, 2)
    mom_in = fetch(mom_h, mom_v, 3)
    nears, fars = pl.ds(0, WIDTH), pl.ds(WIDTH, WIDTH)
    w_in = fetch(w_h.at[pl.ds(zh * 4, 4)], w_pair.at[:, :, :, :, nears], 4)
    rest_in = fetch(rest_h, rest_ref, 5)
    pick_in = fetch(pick_h, pick_ref, 6)
    cot_in = fetch(cot_h, cot_ref, 7)

    outgoing = []

    def go(copy):
        copy.start()
        outgoing.append(copy)
        return copy

    def spectrum(j):
        cols = slice(j * CHUNK, (j + 1) * CHUNK)
        spectra_own[:, cols] = jnp.dot(
            gathered[0], basis_ref[:, cols], preferred_element_type=F32
        ).astype(BF16)

    def code_tokens(slot):
        for j in range(COLS // CHUNK):
            coded = lax.dot_general(
                coder_ref[...], gathered[slot, :, j * CHUNK:(j + 1) * CHUNK],
                (((1,), (1,)), ((), ())), preferred_element_type=F32,
            ).astype(BF16)
            high_t[pl.ds(slot * COLS + j * CHUNK, CHUNK), :] = coded[:CHUNK]
            low_t[pl.ds(slot * CODED + j * SPAN, SPAN), :] = coded[CHUNK:]

    def low_far(i):
        low_t[pl.ds((4 + i) * CODED, CODED), :] = lax.dot_general(
            pick_ref[...], spectra[i, :, :FIRST],
            (((1,), (1,)), ((), ())), preferred_element_type=F32,
        ).astype(BF16)

    def high_far(i):
        for j in range(COLS // CHUNK):
            high_t[pl.ds((4 + i) * COLS + j * CHUNK, CHUNK), :] = lax.dot_general(
                rest_ref[j * CHUNK:(j + 1) * CHUNK, :], spectra[i],
                (((1,), (1,)), ((), ())), preferred_element_type=F32,
            ).astype(BF16)

    def add_hidden(slot, rows):
        hidden[rows, :] += jnp.dot(
            gathered[slot, rows, :], w_pair[places[slot]].reshape(COLS, 2 * WIDTH),
            preferred_element_type=F32,
        )

    def momentum_pre(slot):
        for j in range(COLS // CHUNK):
            rows = pl.ds(pl.multiple_of(shard[slot] * COLS + j * CHUNK, CHUNK), CHUNK)
            coded = DECAY * jnp.dot(
                coder_ref[...], mom_v[rows, :].astype(BF16), preferred_element_type=F32
            )
            mom_out[pl.ds(slot * COLS + j * CHUNK, CHUNK), :] = coded[:CHUNK]
            low_pre[pl.ds(slot * CODED + j * SPAN, SPAN), :] = coded[CHUNK:]

    hidden[...] = jnp.zeros_like(hidden)
    tok_in.wait()
    basis_in.wait()
    for j in range(COLS // CHUNK):
        spectrum(j)

    pl.semaphore_wait(barrier, len(partners))

    half = TOK // 2
    halves = [pl.ds(0, half), pl.ds(half, half)]
    upper = [pl.ds(0, half // 2), pl.ds(half, half // 2)]
    lower = [pl.ds(half // 2, half // 2), pl.ds(half + half // 2, half // 2)]
    piece = 64
    pieces = TOK // piece
    lows, highs = pl.ds(0, FIRST), pl.ds(FIRST, COLS - FIRST)

    w_z = go(remote(w_h.at[pl.ds(zo * 4, 4), x, c], w_pair.at[:, x, c, :, fars], far))
    from_l = [go(remote(tok_h.at[halves[0]], gathered.at[1, halves[0]], right))]
    from_r = [go(remote(tok_h.at[halves[0]], gathered.at[2, halves[0]], left))]
    coder_in.wait()
    code_tokens(0)
    mom_in.wait()
    for s in range(4):
        momentum_pre(s)
    low_z = go(remote(spectra_own.at[:, lows], spectra.at[0, :, lows], far))
    high_z, high_r, high_l, high_o = [], [], [], []

    def send_high():
        rows = pl.ds(len(high_z) * piece, piece)
        high_z.append(go(remote(spectra_own.at[rows, highs], spectra.at[0, rows, highs], far)))

    def forward_high(i):
        rows = pl.ds(i * piece, piece)
        high_z[i].wait_recv()
        high_r.append(go(remote(spectra.at[0, rows, highs], spectra.at[1, rows, highs], right)))
        high_l.append(go(remote(spectra.at[0, rows, highs], spectra.at[2, rows, highs], left)))

    def forward_high_opp(i):
        one = pl.ds(i * piece, piece // 2)
        two = pl.ds(i * piece + piece // 2, piece // 2)
        high_r[i].wait_recv()
        high_o.append(go(remote(spectra.at[1, one, highs], spectra.at[3, one, highs], right)))
        high_l[i].wait_recv()
        high_o.append(go(remote(spectra.at[2, two, highs], spectra.at[3, two, highs], left)))

    send_high()
    for s in range(4, 8):
        momentum_pre(s)
    from_l.append(go(remote(tok_h.at[halves[1]], gathered.at[1, halves[1]], right)))
    from_r.append(go(remote(tok_h.at[halves[1]], gathered.at[2, halves[1]], left)))
    w_z.wait_recv()
    share = w_pair.at[:, x, c, :, fars]
    w_x = [go(remote(share, share, p)) for p in x_peers]
    from_o = []

    def forward_tokens(i):
        from_l[i].wait_recv()
        from_o.append(go(remote(gathered.at[1, upper[i]], gathered.at[3, upper[i]], right)))
        from_r[i].wait_recv()
        from_o.append(go(remote(gathered.at[2, lower[i]], gathered.at[3, lower[i]], left)))

    forward_tokens(0)
    send_high()
    send_high()
    for copy in w_x:
        copy.wait_recv()
    share = w_pair.at[:, :, c, :, fars]
    w_core = go(remote(share, share, sibling))
    forward_tokens(1)
    code_tokens(1)
    code_tokens(2)
    w_in.wait()
    w_core.wait_recv()
    for s in range(3):
        add_hidden(s, halves[0])
    from_o[0].wait_recv()
    from_o[1].wait_recv()
    add_hidden(3, halves[0])
    hidden_z = []

    def send_hidden(i):
        give_far[halves[i], :] = hidden[halves[i], fars].astype(BF16)
        hidden_z.append(go(remote(give_far.at[halves[i]], take_far.at[halves[i]], far)))

    send_hidden(0)
    for s in range(3):
        add_hidden(s, halves[1])
    low_z.wait_recv()
    from_o[2].wait_recv()
    from_o[3].wait_recv()
    low_r = [go(remote(spectra.at[0, halves[0], lows], spectra.at[1, halves[0], lows], right))]
    low_l = [go(remote(spectra.at[0, halves[0], lows], spectra.at[2, halves[0], lows], left))]
    add_hidden(3, halves[1])
    send_hidden(1)
    low_r.append(go(remote(spectra.at[0, halves[1], lows], spectra.at[1, halves[1], lows], right)))
    low_l.append(go(remote(spectra.at[0, halves[1], lows], spectra.at[2, halves[1], lows], left)))
    send_high()
    send_high()
    code_tokens(3)
    pick_in.wait()
    low_far(0)
    low_o = []
    for i in range(2):
        low_r[i].wait_recv()
        low_o.append(go(remote(spectra.at[1, upper[i], lows], spectra.at[3, upper[i], lows], right)))
        low_l[i].wait_recv()
        low_o.append(go(remote(spectra.at[2, lower[i], lows], spectra.at[3, lower[i], lows], left)))
    forward_high(0)
    mirror = [0, 2, 1, 3]
    near = [None, left, right, opp]
    rows_y = [
        go(remote(w_pair.at[places[s], x, c], w_rows.at[mirror[s] - 1, x, c], near[s]))
        for s in range(1, 4)
    ]
    low_far(1)
    low_far(2)
    cot_in.wait()
    for copy in hidden_z:
        copy.wait_recv()

    h = hidden[:, nears] + take_far[...].astype(F32)
    sig = jax.nn.sigmoid(h)
    act[0, :, nears] = (cot_ref[...].astype(F32) * sig * (1.0 + h * (1.0 - sig))).astype(BF16)
    act_z = go(remote(act.at[0, :, nears], act.at[0, :, fars], far))

    inv = 1.0 / math.sqrt(TOK)

    def code(slot):
        rows = pl.ds(pl.multiple_of(slot * CODED, CODED), CODED)
        grad = jnp.dot(low_t[rows, :], act[0, :, nears], preferred_element_type=F32)
        return low_pre[rows, :] + grad * inv

    def momentum_post(slot):
        rows = pl.ds(slot * COLS, COLS)
        grad = jnp.dot(high_t[rows, :], act[0, :, nears], preferred_element_type=F32)
        mom_out[rows, :] = mom_out[rows, :] + grad * inv

    for copy in low_o:
        copy.wait_recv()
    forward_high(1)
    forward_high(2)
    low_far(3)
    order = [xs[1], xs[0], xs[2], x]
    peers_of = [x_peers[1], x_peers[0], x_peers[2]]
    red_core = []
    for i, v in enumerate(order):
        to_core[i] = code((1 - c) * 4 + v).astype(BF16)
        red_core.append(go(remote(to_core.at[i], from_core.at[i], sibling)))
    red_x = []
    for i, v in enumerate(order):
        own = code(c * 4 + v)
        red_core[i].wait_recv()
        both = own + from_core[i].astype(F32)
        if i < 3:
            part_x[i] = both.astype(BF16)
            red_x.append(go(remote(part_x.at[i], from_x.at[i], peers_of[i])))
        else:
            kept_x[...] = both
    act_l = go(remote(act.at[0, :, nears], act.at[1, :, nears], right))
    act_r = go(remote(act.at[0, :, nears], act.at[2, :, nears], left))
    act_o = go(remote(act.at[0, :, nears], act.at[3, :, nears], opp))
    for s in range(4):
        momentum_post(s)
    forward_high(3)
    for copy in red_x:
        copy.wait_recv()
    part_z[...] = (
        kept_x[...] + from_x[0].astype(F32) + from_x[1].astype(F32) + from_x[2].astype(F32)
    ).reshape(4, 48, WIDTH)
    to_z[...] = part_z[...].astype(BF16)
    red_z = [
        go(remote(to_z.at[v], from_z.at[i], p)) for i, (v, p) in enumerate(zip(zs, z_peers))
    ]
    for copy in rows_y:
        copy.wait_recv()
    share = w_rows.at[:, x, c]
    rows_x = [go(remote(share, share, p)) for p in x_peers]
    forward_high(4)
    act_z.wait_recv()
    act_fl = go(remote(act.at[0, :, fars], act.at[1, :, fars], right))
    act_fr = go(remote(act.at[0, :, fars], act.at[2, :, fars], left))
    act_fo = go(remote(act.at[0, :, fars], act.at[3, :, fars], opp))
    for copy in red_z:
        copy.wait_recv()
    tot_out[c, x, zl] = (
        part_z[zl] + from_z[0].astype(F32) + from_z[1].astype(F32) + from_z[2].astype(F32)
    ).astype(BF16)
    piece_ref = tot_out.at[c, x, zl]
    spread_z = [go(remote(piece_ref, piece_ref, p)) for p in z_peers]
    spread_x = [[go(remote(piece_ref, piece_ref, p)) for p in x_peers]]
    rest_in.wait()
    high_far(0)
    momentum_post(4)
    for i in range(2):
        forward_high_opp(i)
    for i in range(3):
        spread_z[i].wait_recv()
        got = tot_out.at[c, x, zs[2 - i]]
        spread_x.append([go(remote(got, got, p)) for p in x_peers])
    quarter = tot_out.at[c, x]
    spread_core = [go(remote(quarter, quarter, sibling))]
    for i in range(2, 5):
        forward_high_opp(i)
    for copy in rows_x:
        copy.wait_recv()
    rows_core = go(remote(w_rows.at[:, :, c], w_rows.at[:, :, c], sibling))
    high_far(1)
    momentum_post(5)
    for i in range(3):
        for copies in spread_x:
            copies[i].wait_recv()
        got = tot_out.at[c, xs[2 - i]]
        spread_core.append(go(remote(got, got, sibling)))
    high_far(2)
    momentum_post(6)
    for copy in high_o:
        copy.wait_recv()
    high_far(3)
    momentum_post(7)
    for copy in [rows_core, act_l, act_r, act_o, act_fl, act_fr, act_fo]:
        copy.wait_recv()

    def weight_rows(s):
        block = w_pair[y] if s == 0 else w_rows[s - 1]
        return block.reshape(COLS, 2 * WIDTH)

    for j in range(COLS // CHUNK):
        cols = slice(j * CHUNK, (j + 1) * CHUNK)
        acc = jnp.zeros((TOK, CHUNK), F32)
        for s in range(4):
            acc = acc + lax.dot_general(
                act[s], weight_rows(s)[cols], (((1,), (1,)), ((), ())),
                preferred_element_type=F32,
            )
        grad_out[:, cols] = acc.astype(BF16)

    for copy in spread_core:
        copy.wait_recv()
    for copy in outgoing:
        copy.wait_send()


def write_kernel(scale, grad_ref, mom_ref, total_ref, decoder_ref, grad_out, mom_out, upd_out, update, sems):
    x, y, zh, zl, c = position()
    zo = 1 - zh
    ys = (y, (y + 3) % 4, (y + 1) % 4, (y + 2) % 4)
    shard = [zh * 4 + v for v in ys] + [zo * 4 + v for v in ys]
    copies = []

    def put(src, dst):
        copies.append(pltpu.make_async_copy(src, dst, sems.at[len(copies)]))
        copies[-1].start()

    for s in range(8):
        rows = pl.ds(pl.multiple_of(shard[s] * COLS, COLS), COLS)
        put(mom_ref.at[pl.ds(s * COLS, COLS)], mom_out.at[0, rows])
    put(grad_ref, grad_out)
    for s in range(8):
        coded = total_ref[s // 4, s % 4].reshape(CODED, WIDTH)
        for j in range(COLS // CHUNK):
            update[pl.ds(s * COLS + j * CHUNK, CHUNK), :] = scale * jnp.dot(
                decoder_ref[...], coded[j * SPAN:(j + 1) * SPAN], preferred_element_type=F32
            )
        rows = pl.ds(pl.multiple_of(shard[s] * COLS, COLS), COLS)
        put(update.at[pl.ds(s * COLS, COLS)], upd_out.at[rows])
    for copy in copies:
        copy.wait()


def per_device(tokens, cotangent, weights, momentum):
    replicas = lax.axis_size("replica")

    def constant(values):
        return jnp.asarray(values, F32).astype(BF16)

    basis = shard_basis()
    rest = np.where(np.arange(COLS)[None, :] < CODED, 0.0, basis)
    pick = np.eye(CODED, FIRST)
    decoder_c = constant(decoder())
    vmem = pl.BlockSpec(memory_space=pltpu.VMEM)
    hbm = pl.BlockSpec(memory_space=pltpu.HBM)
    copies = 120
    split = (4, 2, 96, WIDTH)
    pair = (4, 2, 96, 2 * WIDTH)
    input_grad, momentum_out, total = pl.pallas_call(
        step_kernel,
        out_shape=(
            pltpu.VMEM((TOK, COLS), BF16),
            pltpu.VMEM((D, WIDTH), F32),
            pltpu.VMEM((2, 4, 4, 48, WIDTH), BF16),
        ),
        in_specs=[hbm] * 8,
        out_specs=(vmem, vmem, vmem),
        scratch_shapes=[
            pltpu.VMEM((CHUNK + SPAN, CHUNK), BF16),
            pltpu.VMEM((COLS, COLS), BF16),
            pltpu.VMEM((COLS, COLS), BF16),
            pltpu.VMEM((CODED, FIRST), BF16),
            pltpu.VMEM((TOK, WIDTH), BF16),
            pltpu.VMEM((4, TOK, COLS), BF16),
            pltpu.VMEM((TOK, COLS), BF16),
            pltpu.VMEM((4, TOK, COLS), BF16),
            pltpu.VMEM((4,) + pair, BF16),
            pltpu.VMEM((3,) + pair, BF16),
            pltpu.VMEM((D, WIDTH), F32),
            pltpu.VMEM((D, TOK), BF16),
            pltpu.VMEM((8 * CODED, TOK), BF16),
            pltpu.VMEM((8 * CODED, WIDTH), F32),
            pltpu.VMEM((TOK, 2 * WIDTH), F32),
            pltpu.VMEM((TOK, WIDTH), BF16),
            pltpu.VMEM((TOK, WIDTH), BF16),
            pltpu.VMEM((4, TOK, 2 * WIDTH), BF16),
            pltpu.VMEM((4, CODED, WIDTH), BF16),
            pltpu.VMEM((4, CODED, WIDTH), BF16),
            pltpu.VMEM((3, CODED, WIDTH), BF16),
            pltpu.VMEM((CODED, WIDTH), F32),
            pltpu.VMEM((3, CODED, WIDTH), BF16),
            pltpu.VMEM((4, 48, WIDTH), F32),
            pltpu.VMEM((4, 48, WIDTH), BF16),
            pltpu.VMEM((3, 48, WIDTH), BF16),
            pltpu.SemaphoreType.DMA((copies,)),
            pltpu.SemaphoreType.DMA((copies,)),
            pltpu.SemaphoreType.DMA((8,)),
        ],
        compiler_params=pltpu.CompilerParams(
            collective_id=0, has_side_effects=True, vmem_limit_bytes=52 << 20
        ),
        name="step",
    )(
        tokens, cotangent, weights.reshape((8,) + split), momentum[0],
        constant(coder()), constant(basis), constant(rest), constant(pick),
    )
    return pl.pallas_call(
        lambda *refs: write_kernel(1.0 / math.sqrt(replicas), *refs),
        out_shape=(
            jax.ShapeDtypeStruct((TOK, COLS), BF16),
            jax.ShapeDtypeStruct((1, D, WIDTH), F32),
            jax.ShapeDtypeStruct((D, WIDTH), F32),
        ),
        in_specs=[vmem] * 4,
        out_specs=(hbm, hbm, hbm),
        scratch_shapes=[pltpu.VMEM((D, WIDTH), F32), pltpu.SemaphoreType.DMA((17,))],
        compiler_params=pltpu.CompilerParams(vmem_limit_bytes=16 << 20),
        name="write",
    )(input_grad, momentum_out, total, decoder_c)


def solution(mesh):
    in_specs = (
        P("replica", "tensor"),
        P("replica", "tensor"),
        P(None, "tensor"),
        P("replica", None, "tensor"),
    )
    out_specs = (P("replica", "tensor"), P("replica", None, "tensor"), P(None, "tensor"))
    return jax.shard_map(
        per_device, mesh=mesh, in_specs=in_specs, out_specs=out_specs, check_vma=False
    )
```

```python
import math

import jax
import jax.numpy as jnp
import numpy as np
from jax import lax
from jax.experimental import pallas as pl
from jax.experimental.pallas import tpu as pltpu
from jax.sharding import PartitionSpec as P

SPAN = 64
KEEP = 16
D = 6144
TOK = 320
COLS = 768
WIDTH = 128
CODED = 192
CHUNK = 256
FIRST = 256
DECAY = 0.9
MESH = pl.DeviceIdType.MESH
F32 = jnp.float32
BF16 = jnp.bfloat16


def cosine_basis():
    order = np.arange(SPAN, dtype=np.float64)[:, None]
    place = np.arange(SPAN, dtype=np.float64)[None, :]
    table = np.cos(np.pi * (place + 0.5) * order / SPAN) * math.sqrt(2.0 / SPAN)
    return np.where(order == 0, table * math.sqrt(0.5), table)


def cosine_table():
    return cosine_basis()[:KEEP]


def shard_basis():
    blocks = np.kron(np.eye(COLS // SPAN), cosine_basis().T).reshape(COLS, COLS // SPAN, SPAN)
    kept = blocks[:, :, :KEEP].reshape(COLS, -1)
    others = blocks[:, :, KEEP:].reshape(COLS, -1)
    return np.concatenate([kept, others], axis=1)


def coder():
    table = cosine_table()
    four = np.eye(CHUNK // SPAN)
    rest = np.kron(four, np.eye(SPAN) - table.T @ table)
    return np.concatenate([rest, np.kron(four, table)], axis=0)


def decoder():
    return np.kron(np.eye(CHUNK // SPAN), cosine_table().T)


def position():
    t = lax.axis_index("tensor")
    r = lax.axis_index("replica")
    return r // 8, t % 4, t // 4, (r // 2) % 4, r % 2


def device(x, y, zh, zl, c):
    return (zh * 4 + y, (x * 4 + zl) * 2 + c)


def step_kernel(
    tok_h, cot_h, w_h, mom_h, coder_h, basis_h, rest_h, pick_h,
    grad_out, mom_out, tot_out,
    coder_ref, basis_ref, rest_ref, pick_ref, cot_ref,
    gathered, spectra_own, spectra, w_pair, w_rows, mom_v, high_t, low_t, low_pre,
    hidden, give_far, take_far, act,
    to_core, from_core, part_x, kept_x, from_x, part_z, to_z, from_z,
    send, recv, local,
):
    x, y, zh, zl, c = position()
    yr, yl, yo = (y + 1) % 4, (y + 3) % 4, (y + 2) % 4
    zo = 1 - zh
    right, left, opp = device(x, yr, zh, zl, c), device(x, yl, zh, zl, c), device(x, yo, zh, zl, c)
    far = device(x, y, zo, zl, c)
    sibling = device(x, y, zh, zl, 1 - c)
    xs = [(x + d) % 4 for d in (1, 2, 3)]
    zs = [(zl + d) % 4 for d in (1, 2, 3)]
    x_peers = [device(v, y, zh, zl, c) for v in xs]
    z_peers = [device(x, y, zh, v, c) for v in zs]
    places = (y, yl, yr, yo)
    shard = [zh * 4 + v for v in places] + [zo * 4 + v for v in places]
    counter = iter(range(1000))

    def remote(src, dst, target):
        k = next(counter)
        return pltpu.make_async_remote_copy(
            src_ref=src, dst_ref=dst, send_sem=send.at[k], recv_sem=recv.at[k],
            device_id=target, device_id_type=MESH,
        )

    barrier = pltpu.get_barrier_semaphore()
    partners = [right, left, opp, far, sibling] + x_peers + z_peers
    for p in partners:
        pl.semaphore_signal(barrier, inc=1, device_id=p, device_id_type=MESH)

    def fetch(src, dst, k):
        copy = pltpu.make_async_copy(src, dst, local.at[k])
        copy.start()
        return copy

    tok_in = fetch(tok_h, gathered.at[0], 0)
    basis_in = fetch(basis_h, basis_ref, 1)
    coder_in = fetch(coder_h, coder_ref, 2)
    mom_in = fetch(mom_h, mom_v, 3)
    nears, fars = pl.ds(0, WIDTH), pl.ds(WIDTH, WIDTH)
    w_in = fetch(w_h.at[pl.ds(zh * 4, 4)], w_pair.at[:, :, :, :, nears], 4)
    rest_in = fetch(rest_h, rest_ref, 5)
    pick_in = fetch(pick_h, pick_ref, 6)
    cot_in = fetch(cot_h, cot_ref, 7)

    outgoing = []

    def go(copy):
        copy.start()
        outgoing.append(copy)
        return copy

    def spectrum(j):
        cols = slice(j * CHUNK, (j + 1) * CHUNK)
        spectra_own[:, cols] = jnp.dot(
            gathered[0], basis_ref[:, cols], preferred_element_type=F32
        ).astype(BF16)

    def code_tokens(slot):
        for j in range(COLS // CHUNK):
            coded = lax.dot_general(
                coder_ref[...], gathered[slot, :, j * CHUNK:(j + 1) * CHUNK],
                (((1,), (1,)), ((), ())), preferred_element_type=F32,
            ).astype(BF16)
            high_t[pl.ds(slot * COLS + j * CHUNK, CHUNK), :] = coded[:CHUNK]
            low_t[pl.ds(slot * CODED + j * SPAN, SPAN), :] = coded[CHUNK:]

    def low_far(i):
        low_t[pl.ds((4 + i) * CODED, CODED), :] = lax.dot_general(
            pick_ref[...], spectra[i, :, :FIRST],
            (((1,), (1,)), ((), ())), preferred_element_type=F32,
        ).astype(BF16)

    def high_far(i):
        for j in range(COLS // CHUNK):
            high_t[pl.ds((4 + i) * COLS + j * CHUNK, CHUNK), :] = lax.dot_general(
                rest_ref[j * CHUNK:(j + 1) * CHUNK, :], spectra[i],
                (((1,), (1,)), ((), ())), preferred_element_type=F32,
            ).astype(BF16)

    def add_hidden(slot, rows):
        hidden[rows, :] += jnp.dot(
            gathered[slot, rows, :], w_pair[places[slot]].reshape(COLS, 2 * WIDTH),
            preferred_element_type=F32,
        )

    def momentum_pre(slot):
        for j in range(COLS // CHUNK):
            rows = pl.ds(pl.multiple_of(shard[slot] * COLS + j * CHUNK, CHUNK), CHUNK)
            coded = DECAY * jnp.dot(
                coder_ref[...], mom_v[rows, :].astype(BF16), preferred_element_type=F32
            )
            mom_out[pl.ds(slot * COLS + j * CHUNK, CHUNK), :] = coded[:CHUNK]
            low_pre[pl.ds(slot * CODED + j * SPAN, SPAN), :] = coded[CHUNK:]

    hidden[...] = jnp.zeros_like(hidden)
    tok_in.wait()
    basis_in.wait()
    for j in range(COLS // CHUNK):
        spectrum(j)

    pl.semaphore_wait(barrier, len(partners))

    half = TOK // 2
    halves = [pl.ds(0, half), pl.ds(half, half)]
    upper = [pl.ds(0, half // 2), pl.ds(half, half // 2)]
    lower = [pl.ds(half // 2, half // 2), pl.ds(half + half // 2, half // 2)]
    piece = 64
    pieces = TOK // piece
    lows, highs = pl.ds(0, FIRST), pl.ds(FIRST, COLS - FIRST)

    w_z = go(remote(w_h.at[pl.ds(zo * 4, 4), x, c], w_pair.at[:, x, c, :, fars], far))
    from_l = [go(remote(tok_h.at[halves[0]], gathered.at[1, halves[0]], right))]
    from_r = [go(remote(tok_h.at[halves[0]], gathered.at[2, halves[0]], left))]
    coder_in.wait()
    code_tokens(0)
    mom_in.wait()
    for s in range(4):
        momentum_pre(s)
    low_z = go(remote(spectra_own.at[:, lows], spectra.at[0, :, lows], far))
    high_z, high_r, high_l, high_o = [], [], [], []

    def send_high():
        rows = pl.ds(len(high_z) * piece, piece)
        high_z.append(go(remote(spectra_own.at[rows, highs], spectra.at[0, rows, highs], far)))

    def forward_high(i):
        rows = pl.ds(i * piece, piece)
        high_z[i].wait_recv()
        high_r.append(go(remote(spectra.at[0, rows, highs], spectra.at[1, rows, highs], right)))
        high_l.append(go(remote(spectra.at[0, rows, highs], spectra.at[2, rows, highs], left)))

    def forward_high_opp(i):
        one = pl.ds(i * piece, piece // 2)
        two = pl.ds(i * piece + piece // 2, piece // 2)
        high_r[i].wait_recv()
        high_o.append(go(remote(spectra.at[1, one, highs], spectra.at[3, one, highs], right)))
        high_l[i].wait_recv()
        high_o.append(go(remote(spectra.at[2, two, highs], spectra.at[3, two, highs], left)))

    send_high()
    for s in range(4, 8):
        momentum_pre(s)
    from_l.append(go(remote(tok_h.at[halves[1]], gathered.at[1, halves[1]], right)))
    from_r.append(go(remote(tok_h.at[halves[1]], gathered.at[2, halves[1]], left)))
    w_z.wait_recv()
    share = w_pair.at[:, x, c, :, fars]
    w_x = [go(remote(share, share, p)) for p in x_peers]
    from_o = []

    def forward_tokens(i):
        from_l[i].wait_recv()
        from_o.append(go(remote(gathered.at[1, upper[i]], gathered.at[3, upper[i]], right)))
        from_r[i].wait_recv()
        from_o.append(go(remote(gathered.at[2, lower[i]], gathered.at[3, lower[i]], left)))

    forward_tokens(0)
    send_high()
    send_high()
    for copy in w_x:
        copy.wait_recv()
    share = w_pair.at[:, :, c, :, fars]
    w_core = go(remote(share, share, sibling))
    forward_tokens(1)
    code_tokens(1)
    code_tokens(2)
    w_in.wait()
    w_core.wait_recv()
    for s in range(3):
        add_hidden(s, halves[0])
    from_o[0].wait_recv()
    from_o[1].wait_recv()
    add_hidden(3, halves[0])
    hidden_z = []

    def send_hidden(i):
        give_far[halves[i], :] = hidden[halves[i], fars].astype(BF16)
        hidden_z.append(go(remote(give_far.at[halves[i]], take_far.at[halves[i]], far)))

    send_hidden(0)
    for s in range(3):
        add_hidden(s, halves[1])
    low_z.wait_recv()
    from_o[2].wait_recv()
    from_o[3].wait_recv()
    low_r = [go(remote(spectra.at[0, halves[0], lows], spectra.at[1, halves[0], lows], right))]
    low_l = [go(remote(spectra.at[0, halves[0], lows], spectra.at[2, halves[0], lows], left))]
    add_hidden(3, halves[1])
    send_hidden(1)
    low_r.append(go(remote(spectra.at[0, halves[1], lows], spectra.at[1, halves[1], lows], right)))
    low_l.append(go(remote(spectra.at[0, halves[1], lows], spectra.at[2, halves[1], lows], left)))
    send_high()
    send_high()
    code_tokens(3)
    pick_in.wait()
    low_far(0)
    low_o = []
    for i in range(2):
        low_r[i].wait_recv()
        low_o.append(go(remote(spectra.at[1, upper[i], lows], spectra.at[3, upper[i], lows], right)))
        low_l[i].wait_recv()
        low_o.append(go(remote(spectra.at[2, lower[i], lows], spectra.at[3, lower[i], lows], left)))
    forward_high(0)
    mirror = [0, 2, 1, 3]
    near = [None, left, right, opp]
    rows_y = [
        go(remote(w_pair.at[places[s], x, c], w_rows.at[mirror[s] - 1, x, c], near[s]))
        for s in range(1, 4)
    ]
    low_far(1)
    low_far(2)
    cot_in.wait()
    for copy in hidden_z:
        copy.wait_recv()

    h = hidden[:, nears] + take_far[...].astype(F32)
    sig = jax.nn.sigmoid(h)
    act[0, :, nears] = (cot_ref[...].astype(F32) * sig * (1.0 + h * (1.0 - sig))).astype(BF16)
    act_z = go(remote(act.at[0, :, nears], act.at[0, :, fars], far))

    inv = 1.0 / math.sqrt(TOK)

    def code(slot):
        rows = pl.ds(pl.multiple_of(slot * CODED, CODED), CODED)
        grad = jnp.dot(low_t[rows, :], act[0, :, nears], preferred_element_type=F32)
        return low_pre[rows, :] + grad * inv

    def momentum_post(slot):
        rows = pl.ds(slot * COLS, COLS)
        grad = jnp.dot(high_t[rows, :], act[0, :, nears], preferred_element_type=F32)
        mom_out[rows, :] = mom_out[rows, :] + grad * inv

    for copy in low_o:
        copy.wait_recv()
    forward_high(1)
    forward_high(2)
    low_far(3)
    order = [xs[1], xs[0], xs[2], x]
    peers_of = [x_peers[1], x_peers[0], x_peers[2]]
    red_core = []
    for i, v in enumerate(order):
        to_core[i] = code((1 - c) * 4 + v).astype(BF16)
        red_core.append(go(remote(to_core.at[i], from_core.at[i], sibling)))
    red_x = []
    for i, v in enumerate(order):
        own = code(c * 4 + v)
        red_core[i].wait_recv()
        both = own + from_core[i].astype(F32)
        if i < 3:
            part_x[i] = both.astype(BF16)
            red_x.append(go(remote(part_x.at[i], from_x.at[i], peers_of[i])))
        else:
            kept_x[...] = both
    act_l = go(remote(act.at[0, :, nears], act.at[1, :, nears], right))
    act_r = go(remote(act.at[0, :, nears], act.at[2, :, nears], left))
    act_o = go(remote(act.at[0, :, nears], act.at[3, :, nears], opp))
    for s in range(4):
        momentum_post(s)
    forward_high(3)
    for copy in red_x:
        copy.wait_recv()
    part_z[...] = (
        kept_x[...] + from_x[0].astype(F32) + from_x[1].astype(F32) + from_x[2].astype(F32)
    ).reshape(4, 48, WIDTH)
    to_z[...] = part_z[...].astype(BF16)
    red_z = [
        go(remote(to_z.at[v], from_z.at[i], p)) for i, (v, p) in enumerate(zip(zs, z_peers))
    ]
    for copy in rows_y:
        copy.wait_recv()
    share = w_rows.at[:, x, c]
    rows_x = [go(remote(share, share, p)) for p in x_peers]
    forward_high(4)
    act_z.wait_recv()
    act_fl = go(remote(act.at[0, :, fars], act.at[1, :, fars], right))
    act_fr = go(remote(act.at[0, :, fars], act.at[2, :, fars], left))
    act_fo = go(remote(act.at[0, :, fars], act.at[3, :, fars], opp))
    for copy in red_z:
        copy.wait_recv()
    tot_out[c, x, zl] = (
        part_z[zl] + from_z[0].astype(F32) + from_z[1].astype(F32) + from_z[2].astype(F32)
    ).astype(BF16)
    piece_ref = tot_out.at[c, x, zl]
    spread_z = [go(remote(piece_ref, piece_ref, p)) for p in z_peers]
    spread_x = [[go(remote(piece_ref, piece_ref, p)) for p in x_peers]]
    rest_in.wait()
    high_far(0)
    momentum_post(4)
    for i in range(2):
        forward_high_opp(i)
    for i in range(3):
        spread_z[i].wait_recv()
        got = tot_out.at[c, x, zs[2 - i]]
        spread_x.append([go(remote(got, got, p)) for p in x_peers])
    quarter = tot_out.at[c, x]
    spread_core = [go(remote(quarter, quarter, sibling))]
    for i in range(2, 5):
        forward_high_opp(i)
    for copy in rows_x:
        copy.wait_recv()
    rows_core = go(remote(w_rows.at[:, :, c], w_rows.at[:, :, c], sibling))
    high_far(1)
    momentum_post(5)
    for i in range(3):
        for copies in spread_x:
            copies[i].wait_recv()
        got = tot_out.at[c, xs[2 - i]]
        spread_core.append(go(remote(got, got, sibling)))
    high_far(2)
    momentum_post(6)
    for copy in [rows_core, act_l, act_r, act_o, act_fl, act_fr, act_fo]:
        copy.wait_recv()

    def weight_rows(s):
        block = w_pair[y] if s == 0 else w_rows[s - 1]
        return block.reshape(COLS, 2 * WIDTH)

    for j in range(COLS // CHUNK):
        cols = slice(j * CHUNK, (j + 1) * CHUNK)
        acc = jnp.zeros((TOK, CHUNK), F32)
        for s in range(4):
            acc = acc + lax.dot_general(
                act[s], weight_rows(s)[cols], (((1,), (1,)), ((), ())),
                preferred_element_type=F32,
            )
        grad_out[:, cols] = acc.astype(BF16)

    for copy in high_o:
        copy.wait_recv()
    high_far(3)
    momentum_post(7)
    for copy in spread_core:
        copy.wait_recv()
    for copy in outgoing:
        copy.wait_send()


def write_kernel(scale, grad_ref, mom_ref, total_ref, decoder_ref, grad_out, mom_out, upd_out, update, sems):
    x, y, zh, zl, c = position()
    zo = 1 - zh
    ys = (y, (y + 3) % 4, (y + 1) % 4, (y + 2) % 4)
    shard = [zh * 4 + v for v in ys] + [zo * 4 + v for v in ys]
    copies = []

    def put(src, dst):
        copies.append(pltpu.make_async_copy(src, dst, sems.at[len(copies)]))
        copies[-1].start()

    for s in range(8):
        rows = pl.ds(pl.multiple_of(shard[s] * COLS, COLS), COLS)
        put(mom_ref.at[pl.ds(s * COLS, COLS)], mom_out.at[0, rows])
    put(grad_ref, grad_out)
    for s in range(8):
        coded = total_ref[s // 4, s % 4].reshape(CODED, WIDTH)
        for j in range(COLS // CHUNK):
            update[pl.ds(s * COLS + j * CHUNK, CHUNK), :] = scale * jnp.dot(
                decoder_ref[...], coded[j * SPAN:(j + 1) * SPAN], preferred_element_type=F32
            )
        rows = pl.ds(pl.multiple_of(shard[s] * COLS, COLS), COLS)
        put(update.at[pl.ds(s * COLS, COLS)], upd_out.at[rows])
    for copy in copies:
        copy.wait()


def per_device(tokens, cotangent, weights, momentum):
    replicas = lax.axis_size("replica")

    def constant(values):
        return jnp.asarray(values, F32).astype(BF16)

    basis = shard_basis()
    rest = np.where(np.arange(COLS)[None, :] < CODED, 0.0, basis)
    pick = np.eye(CODED, FIRST)
    decoder_c = constant(decoder())
    vmem = pl.BlockSpec(memory_space=pltpu.VMEM)
    hbm = pl.BlockSpec(memory_space=pltpu.HBM)
    copies = 120
    split = (4, 2, 96, WIDTH)
    pair = (4, 2, 96, 2 * WIDTH)
    input_grad, momentum_out, total = pl.pallas_call(
        step_kernel,
        out_shape=(
            pltpu.VMEM((TOK, COLS), BF16),
            pltpu.VMEM((D, WIDTH), F32),
            pltpu.VMEM((2, 4, 4, 48, WIDTH), BF16),
        ),
        in_specs=[hbm] * 8,
        out_specs=(vmem, vmem, vmem),
        scratch_shapes=[
            pltpu.VMEM((CHUNK + SPAN, CHUNK), BF16),
            pltpu.VMEM((COLS, COLS), BF16),
            pltpu.VMEM((COLS, COLS), BF16),
            pltpu.VMEM((CODED, FIRST), BF16),
            pltpu.VMEM((TOK, WIDTH), BF16),
            pltpu.VMEM((4, TOK, COLS), BF16),
            pltpu.VMEM((TOK, COLS), BF16),
            pltpu.VMEM((4, TOK, COLS), BF16),
            pltpu.VMEM((4,) + pair, BF16),
            pltpu.VMEM((3,) + pair, BF16),
            pltpu.VMEM((D, WIDTH), F32),
            pltpu.VMEM((D, TOK), BF16),
            pltpu.VMEM((8 * CODED, TOK), BF16),
            pltpu.VMEM((8 * CODED, WIDTH), F32),
            pltpu.VMEM((TOK, 2 * WIDTH), F32),
            pltpu.VMEM((TOK, WIDTH), BF16),
            pltpu.VMEM((TOK, WIDTH), BF16),
            pltpu.VMEM((4, TOK, 2 * WIDTH), BF16),
            pltpu.VMEM((4, CODED, WIDTH), BF16),
            pltpu.VMEM((4, CODED, WIDTH), BF16),
            pltpu.VMEM((3, CODED, WIDTH), BF16),
            pltpu.VMEM((CODED, WIDTH), F32),
            pltpu.VMEM((3, CODED, WIDTH), BF16),
            pltpu.VMEM((4, 48, WIDTH), F32),
            pltpu.VMEM((4, 48, WIDTH), BF16),
            pltpu.VMEM((3, 48, WIDTH), BF16),
            pltpu.SemaphoreType.DMA((copies,)),
            pltpu.SemaphoreType.DMA((copies,)),
            pltpu.SemaphoreType.DMA((8,)),
        ],
        compiler_params=pltpu.CompilerParams(
            collective_id=0, has_side_effects=True, vmem_limit_bytes=52 << 20
        ),
        name="step",
    )(
        tokens, cotangent, weights.reshape((8,) + split), momentum[0],
        constant(coder()), constant(basis), constant(rest), constant(pick),
    )
    return pl.pallas_call(
        lambda *refs: write_kernel(1.0 / math.sqrt(replicas), *refs),
        out_shape=(
            jax.ShapeDtypeStruct((TOK, COLS), BF16),
            jax.ShapeDtypeStruct((1, D, WIDTH), F32),
            jax.ShapeDtypeStruct((D, WIDTH), F32),
        ),
        in_specs=[vmem] * 4,
        out_specs=(hbm, hbm, hbm),
        scratch_shapes=[pltpu.VMEM((D, WIDTH), F32), pltpu.SemaphoreType.DMA((17,))],
        compiler_params=pltpu.CompilerParams(vmem_limit_bytes=16 << 20),
        name="write",
    )(input_grad, momentum_out, total, decoder_c)


def solution(mesh):
    in_specs = (
        P("replica", "tensor"),
        P("replica", "tensor"),
        P(None, "tensor"),
        P("replica", None, "tensor"),
    )
    out_specs = (P("replica", "tensor"), P("replica", None, "tensor"), P(None, "tensor"))
    return jax.shard_map(
        per_device, mesh=mesh, in_specs=in_specs, out_specs=out_specs, check_vma=False
    )
```
